256 devices in a mesh: replica: 32 (over x, y, core), fsdp: 8 (over z).
Axes of the slice: x: 4, y: 4, z: 8, core: 2. Of those that a mesh axis runs over, the one named last changes fastest.
Arguments:
- key_delta: float32 [32, 4096, 1024], P('replica', 'fsdp')
- gain_delta: float32 [32, 4096], P('replica', 'fsdp')
- key_params: float32 [4096, 1024], P('fsdp'), may hold values from -6 to 6
- key_moment: float32 [4096, 1024], P('fsdp'), may hold values from -6 to 6
- gain_params: float32 [4096], P('fsdp'), may hold values from 0.1 to 1.9
- gain_moment: float32 [4096], P('fsdp'), may hold values from -6 to 6
Outputs:
- key_new: float32 [4096, 1024], P('fsdp')
- key_moment_new: float32 [4096, 1024], P('fsdp')
- gain_new: float32 [4096], P('fsdp')
- gain_moment_new: float32 [4096], P('fsdp')
The draws below stay inside these ranges and needn't reach their ends.
All inputs are finite; a program needn't handle non-finite values.
Results may differ from the reference program's by a relative error of at most 0.00002.
Values sent between devices are 32-bit elements; how exact they have to be, the bound alone decides.
A program may use at most 64 MiB of HBM per device.

```python
import jax
import jax.numpy as jnp
from jax import lax

D = 4096
KV = 1024
NREP = 32


def scaled_field(key, shape):
    keys = jax.random.split(key, 3)
    rows = shape[1]
    row_scale = 10.0 ** jax.random.uniform(keys[0], (rows,), jnp.float32)
    rising = 1.0 + 2.0 * jnp.arange(rows, dtype=jnp.float32) / (rows - 1)
    scale = (row_scale * rising).reshape((1, rows) + (1,) * (len(shape) - 2))
    if len(shape) == 3:
        scale = scale * 10.0 ** jax.random.uniform(keys[1], (1, 1, shape[2]), jnp.float32)
    values = jax.random.normal(keys[2], shape, jnp.float32)
    return values * scale * 0.1


def draw_key_delta(key, part):
    return scaled_field(jax.random.fold_in(key, 11), (NREP, D, KV))


def draw_gain_delta(key, part):
    return scaled_field(jax.random.fold_in(key, 23), (NREP, D))


def block_levels(rng, dims, cuts, least, largest):
    loudness = 1.0
    for dim, shards_of in cuts:
        heights = jax.random.uniform(jax.random.fold_in(jax.random.fold_in(rng, 6), dim), (shards_of,), jnp.float32, least / len(cuts), largest / len(cuts))
        loudness = loudness * jnp.repeat(jnp.exp(heights), dims[dim] // shards_of).reshape((-1,) + (1,) * (len(dims) - 1 - dim))
    return loudness


def centred(stream_key, dims, scale, limit, shards=(), kind=jnp.bfloat16):
    level = block_levels(stream_key, dims, shards, -0.22, 0.18) if shards else 1.0
    values = jax.random.normal(stream_key, dims, jnp.float32) * scale * level
    return jnp.minimum(jnp.maximum(values, -limit), limit).astype(kind)


def setup_inputs(seed: int = 0) -> dict:
    key_of = jax.random.split(jax.random.key(seed), 7)
    key_delta = draw_key_delta(jax.random.fold_in(key_of[6], 71), 0)
    gain_delta = draw_gain_delta(jax.random.fold_in(key_of[6], 71), 0)
    key_params = centred(key_of[2], (D, KV), 1.0, 6.0, ((0, 8),), jnp.float32)
    key_moment = centred(key_of[3], (D, KV), 1.0, 6.0, ((0, 8),), jnp.float32)
    gain_params = jnp.clip(1.0 + 0.18 * jax.random.normal(key_of[4], (D,), jnp.float32), 0.1, 1.9)
    gain_moment = centred(key_of[5], (D,), 1.0, 6.0, ((0, 8),), jnp.float32)
    return dict(key_delta=key_delta, gain_delta=gain_delta, key_params=key_params, key_moment=key_moment, gain_params=gain_params, gain_moment=gain_moment)


def outer_update(delta_sum, params, moment):
    average = delta_sum / NREP
    moment_new = 0.9 * moment + average
    step_value = average + 0.9 * moment_new
    rms_value = jnp.sqrt(jnp.mean(step_value * step_value) + 1e-06)
    return (params - 0.7 * step_value / rms_value, moment_new)

def reference(key_delta, gain_delta, key_params, key_moment, gain_params, gain_moment):
    key_new, key_moment_new = outer_update(lax.optimization_barrier(jnp.sum(key_delta, axis=0)), key_params, key_moment)
    gain_new, gain_moment_new = outer_update(lax.optimization_barrier(jnp.sum(gain_delta, axis=0)), gain_params, gain_moment)
    return (key_new, key_moment_new, gain_new, gain_moment_new)
```

```python
import functools

import jax
import jax.numpy as jnp
from jax import lax
from jax.experimental import pallas as pl
from jax.experimental.pallas import tpu as pltpu
from jax.sharding import PartitionSpec as P

D = 4096
KV = 1024
NREP = 32
XS, YS, CORES, ZS = 4, 4, 2, 8
ROWS = D // ZS
HALF = ROWS // CORES
CHUNKS = 2
CROWS = HALF // CHUNKS
BROWS = CROWS // 2 // XS
PCOLS = KV // YS
MESH = pl.DeviceIdType.MESH


def update_kernel(
    kd, gd, kp_hbm, km_hbm, gp_hbm, gm_hbm,
    kn_out, kmn_out, gn_out, gmn_out,
    acc, r0, r1, r2, avg, kp, km,
    gd_v, gp_v, gm_v, g_core, g_x, g_y, s_z, s_y, s_x, s_c,
    load_sem, send_sem, sem0, sem1, sem2, sem3, sem4, sem5,
    gsend_sem, gc_sem, gx_sem, gy_sem, ssend_sem, sz_sem, sy_sem, sx_sem, sc_sem,
):
    r = lax.axis_index("replica")
    z = lax.axis_index("fsdp")
    x = r // (YS * CORES)
    y = (r // CORES) % YS
    c = r % CORES

    def at(px, py, pc):
        return ((px * YS + py) * CORES + pc, z)

    sibling = at(x, y, 1 - c)
    xpeer = [at((x + p) % XS, y, c) for p in range(1, XS)]
    ypeer = [at(x, (y + p) % YS, c) for p in range(1, YS)]
    zpeer = [(r, (z + p) % ZS) for p in range(1, ZS)]
    mine = pl.multiple_of(c * HALF, HALF)
    other = pl.multiple_of((1 - c) * HALF, HALF)

    def send(src, dst, ssem, rsem, device):
        cp = pltpu.make_async_remote_copy(
            src_ref=src, dst_ref=dst, send_sem=ssem, recv_sem=rsem,
            device_id=device, device_id_type=MESH,
        )
        cp.start()
        return cp

    loads = [
        pltpu.make_async_copy(kd.at[0, pl.ds(mine, HALF)], acc, load_sem.at[0]),
        pltpu.make_async_copy(gd, gd_v, load_sem.at[1]),
        pltpu.make_async_copy(gm_hbm, gm_v, load_sem.at[2]),
        pltpu.make_async_copy(gp_hbm, gp_v, load_sem.at[3]),
        pltpu.make_async_copy(km_hbm, km, load_sem.at[4]),
        pltpu.make_async_copy(kp_hbm, kp, load_sem.at[5]),
    ]
    for cp in loads:
        cp.start()

    barrier = pltpu.get_barrier_semaphore()
    partners = [sibling] + xpeer + ypeer + zpeer
    for device in partners:
        pl.semaphore_signal(barrier, inc=1, device_id=device, device_id_type=MESH)
    pl.semaphore_wait(barrier, len(partners))

    c0 = []
    for j in range(CHUNKS):
        c0.append(send(
            kd.at[0, pl.ds(other + j * CROWS, CROWS)],
            r0.at[pl.ds(j * CROWS, CROWS)], send_sem.at[0], sem0.at[j], sibling,
        ))
    loads[1].wait()
    gc = send(gd_v, g_core, gsend_sem.at[0], gc_sem, sibling)

    def block(j, o, q):
        return pl.multiple_of(j * CROWS + o * (CROWS // 2) + q * BROWS, 8)

    first = (x, y)
    second = (y, x)
    peers = ((xpeer, ypeer), (ypeer, xpeer))
    order = (1, 0, 2)

    loads[0].wait()
    c1 = {}
    for j in range(CHUNKS):
        c0[j].wait_recv()
        rows = pl.ds(j * CROWS, CROWS)
        acc[rows] = acc[rows] + r0[rows]
        for p in order:
            for o in range(2):
                q = (first[o] + p + 1) % 4
                c1[j, o, p] = send(
                    acc.at[pl.ds(block(j, o, q), BROWS)],
                    r1.at[p, j, o], send_sem.at[1], sem1.at[j, o, p], peers[o][0][p],
                )
        if j == 0:
            gc.wait_recv()
            g_x[x] = gd_v[...] + g_core[...]
            gx = [send(g_x.at[x], g_x.at[x], gsend_sem.at[1], gx_sem.at[p], xpeer[p]) for p in range(3)]
    for cp in gx:
        cp.wait_recv()
    g_y[y] = (g_x[0] + g_x[1]) + (g_x[2] + g_x[3])
    gy = [send(g_y.at[y], g_y.at[y], gsend_sem.at[2], gy_sem.at[p], ypeer[p]) for p in range(3)]

    def cols(q):
        return pl.ds(pl.multiple_of(q * PCOLS, PCOLS), PCOLS)

    c2 = {}
    for j in range(CHUNKS):
        for o in range(2):
            for p in order:
                c1[j, o, p].wait_recv()
            rows = pl.ds(block(j, o, first[o]), BROWS)
            acc[rows] = (acc[rows] + r1[0, j, o]) + (r1[1, j, o] + r1[2, j, o])
            for p in order:
                q = (second[o] + p + 1) % 4
                c2[j, o, p] = send(
                    acc.at[rows, cols(q)],
                    r2.at[p, j, o], send_sem.at[2], sem2.at[j, o, p], peers[o][1][p],
                )

    for cp in gy:
        cp.wait_recv()
    loads[2].wait()
    loads[3].wait()
    loads[4].wait()
    loads[5].wait()
    g_avg = ((g_y[0] + g_y[1]) + (g_y[2] + g_y[3])) * (1.0 / NREP)
    g_mom = 0.9 * gm_v[...] + g_avg
    g_step = g_avg + 0.9 * g_mom
    gmn_out[...] = g_mom
    g_sq = g_step * g_step
    g_part = (g_sq[:, 0:128] + g_sq[:, 128:256]) + (g_sq[:, 256:384] + g_sq[:, 384:512])

    c3 = {}
    k_part = jnp.zeros((1, 128), jnp.float32)
    for j in range(CHUNKS):
        for o in range(2):
            for p in order:
                c2[j, o, p].wait_recv()
            rows = pl.ds(block(j, o, first[o]), BROWS)
            piece = (acc[rows, cols(second[o])] + r2[0, j, o]) + (r2[1, j, o] + r2[2, j, o])
            piece = piece * (1.0 / NREP)
            arows = pl.ds(mine + block(j, o, first[o]), BROWS)
            avg[arows, cols(second[o])] = piece
            for p in order:
                part = avg.at[arows, cols(second[o])]
                c3[j, o, p] = send(part, part, send_sem.at[3], sem3.at[j, o, p], peers[o][1][p])
            step = piece + 0.9 * (0.9 * km[arows, cols(second[o])] + piece)
            sq = step * step
            k_part = k_part + jnp.sum(sq[:, :128] + sq[:, 128:], axis=0, keepdims=True)

    row = lax.broadcasted_iota(jnp.int32, (8, 128), 0)
    s_z[z] = jnp.where(row == 0, k_part, jnp.where(row == 1, g_part, 0.0))
    sz = [send(s_z.at[z], s_z.at[z], ssend_sem.at[0], sz_sem.at[p], zpeer[p]) for p in range(7)]

    c4 = {}
    for j in range(CHUNKS):
        for o in range(2):
            for p in order:
                c3[j, o, p].wait_recv()
            arows = pl.ds(mine + block(j, o, first[o]), BROWS)
            for p in order:
                part = avg.at[arows]
                c4[j, o, p] = send(part, part, send_sem.at[4], sem4.at[j, o, p], peers[o][0][p])

    for cp in sz:
        cp.wait_recv()
    s_y[y] = ((s_z[0] + s_z[1]) + (s_z[2] + s_z[3])) + ((s_z[4] + s_z[5]) + (s_z[6] + s_z[7]))
    sy = [send(s_y.at[y], s_y.at[y], ssend_sem.at[1], sy_sem.at[p], ypeer[p]) for p in range(3)]
    for cp in sy:
        cp.wait_recv()
    s_x[x] = (s_y[0] + s_y[1]) + (s_y[2] + s_y[3])
    sx = [send(s_x.at[x], s_x.at[x], ssend_sem.at[2], sx_sem.at[p], xpeer[p]) for p in range(3)]
    for cp in sx:
        cp.wait_recv()
    s_c[c] = (s_x[0] + s_x[1]) + (s_x[2] + s_x[3])
    sc = send(s_c.at[c], s_c.at[c], ssend_sem.at[3], sc_sem, sibling)

    g_all = (s_y[0] + s_y[0]) * 0.5
    g_total = jnp.sum(g_all[1:2, :])
    g_scale = 0.7 / jnp.sqrt(jnp.full((1, 128), g_total, jnp.float32) / D + 1e-06)
    gn_out[...] = gp_v[...] - g_step * jnp.concatenate([g_scale] * 4, axis=1)

    sc.wait_recv()
    k_total = jnp.sum(s_c[0, 0:1, :] + s_c[1, 0:1, :])
    k_scale = 0.7 / jnp.sqrt(jnp.full((8, 128), k_total, jnp.float32) / (D * KV) + 1e-06)
    k_scale = jnp.concatenate([k_scale] * (KV // 128), axis=1)

    def finish(base, rows):
        def step_rows(i, carry):
            at_rows = pl.ds(pl.multiple_of(base + i * 8, 8), 8)
            a = avg[at_rows]
            m = 0.9 * km[at_rows] + a
            kmn_out[at_rows] = m
            kn_out[at_rows] = kp[at_rows] - (a + 0.9 * m) * k_scale
            return carry
        lax.fori_loop(0, rows // 8, step_rows, 0, unroll=2)

    c5 = []
    for j in range(CHUNKS):
        for o in range(2):
            for p in order:
                c4[j, o, p].wait_recv()
        part = avg.at[pl.ds(mine + j * CROWS, CROWS)]
        c5.append(send(part, part, send_sem.at[0], sem5.at[j], sibling))
        finish(mine + j * CROWS, CROWS)
    for j in range(CHUNKS):
        c5[j].wait_recv()
        finish(other + j * CROWS, CROWS)

    for group in (c0, c1.values(), c2.values(), c3.values(), c4.values(), c5, [gc], gx, gy, sz, sy, sx, [sc]):
        for cp in group:
            cp.wait_send()


def on_device(key_delta, gain_delta, key_params, key_moment, gain_params, gain_moment):
    f32 = jnp.float32
    dma = pltpu.SemaphoreType.DMA
    hbm = pl.BlockSpec(memory_space=pltpu.HBM)
    vmem = pl.BlockSpec(memory_space=pltpu.VMEM)
    gl = ROWS
    kn, kmn, gn, gmn = pl.pallas_call(
        update_kernel,
        out_shape=(
            jax.ShapeDtypeStruct((ROWS, KV), f32),
            jax.ShapeDtypeStruct((ROWS, KV), f32),
            jax.ShapeDtypeStruct((1, gl), f32),
            jax.ShapeDtypeStruct((1, gl), f32),
        ),
        in_specs=[hbm] * 6,
        out_specs=[vmem] * 4,
        scratch_shapes=[
            pltpu.VMEM((HALF, KV), f32),
            pltpu.VMEM((HALF, KV), f32),
            pltpu.VMEM((3, CHUNKS, 2, BROWS, KV), f32),
            pltpu.VMEM((3, CHUNKS, 2, BROWS, PCOLS), f32),
            pltpu.VMEM((ROWS, KV), f32),
            pltpu.VMEM((ROWS, KV), f32),
            pltpu.VMEM((ROWS, KV), f32),
            pltpu.VMEM((1, gl), f32),
            pltpu.VMEM((1, gl), f32),
            pltpu.VMEM((1, gl), f32),
            pltpu.VMEM((1, gl), f32),
            pltpu.VMEM((4, 1, gl), f32),
            pltpu.VMEM((4, 1, gl), f32),
            pltpu.VMEM((8, 8, 128), f32),
            pltpu.VMEM((4, 8, 128), f32),
            pltpu.VMEM((4, 8, 128), f32),
            pltpu.VMEM((2, 8, 128), f32),
            dma((6,)),
            dma((5,)),
            dma((CHUNKS,)),
            dma((CHUNKS, 2, 3)),
            dma((CHUNKS, 2, 3)),
            dma((CHUNKS, 2, 3)),
            dma((CHUNKS, 2, 3)),
            dma((CHUNKS,)),
            dma((3,)),
            dma,
            dma((3,)),
            dma((3,)),
            dma((4,)),
            dma((7,)),
            dma((3,)),
            dma((3,)),
            dma,
        ],
        compiler_params=pltpu.CompilerParams(
            collective_id=0, has_side_effects=True, vmem_limit_bytes=40 << 20
        ),
        name="outer_update",
    )(
        key_delta, gain_delta, key_params, key_moment,
        gain_params.reshape(1, gl), gain_moment.reshape(1, gl),
    )
    return kn, kmn, gn.reshape(gl), gmn.reshape(gl)


def solution(mesh):
    return jax.shard_map(
        on_device,
        mesh=mesh,
        in_specs=(
            P("replica", "fsdp", None),
            P("replica", "fsdp"),
            P("fsdp", None),
            P("fsdp", None),
            P("fsdp"),
            P("fsdp"),
        ),
        out_specs=(P("fsdp", None), P("fsdp", None), P("fsdp"), P("fsdp")),
        check_vma=False,
    )
```

```python
import jax
import jax.numpy as jnp
from jax import lax
from jax.experimental import pallas as pl
from jax.experimental.pallas import tpu as pltpu
from jax.sharding import PartitionSpec as P

D = 4096
KV = 1024
NREP = 32
XS, YS, CORES, ZS = 4, 4, 2, 8
ROWS = D // ZS
HALF = ROWS // CORES
CHUNKS = 2
CROWS = HALF // CHUNKS
BROWS = CROWS // 2 // XS
PCOLS = KV // YS
TAIL = 8
MESH = pl.DeviceIdType.MESH


def comm_kernel(
    kd, gd, kp_hbm, km_hbm, gp_hbm, gm_hbm,
    mom, stp, kp, scale, gn_out, gmn_out,
    acc, r0, r1, r2, avg, km,
    gd_v, gp_v, gm_v, g_core, g_x, g_y, s_z, s_p,
    load_sem, send_sem, sem0, sem1, sem2, sem3, sem4, sem5,
    gsend_sem, gc_sem, gx_sem, gy_sem, ssend_sem, sz_sem, sp_sem,
):
    r = lax.axis_index("replica")
    z = lax.axis_index("fsdp")
    x = r // (YS * CORES)
    y = (r // CORES) % YS
    c = r % CORES

    def at(px, py, pc):
        return ((px * YS + py) * CORES + pc, z)

    sibling = at(x, y, 1 - c)
    xpeer = [at((x + p) % XS, y, c) for p in (1, 2, 3)]
    ypeer = [at(x, (y + p) % YS, c) for p in (1, 2, 3)]
    plane = [at((x + p) % XS, (y + q) % YS, c) for p in range(4) for q in range(4) if p or q]
    column = [
        (at(x, y, (c + q) % 2)[0], (z + p) % ZS) for p in range(ZS) for q in range(2) if p or q
    ]
    mine = pl.multiple_of(c * HALF, HALF)
    other = pl.multiple_of((1 - c) * HALF, HALF)

    def send(src, dst, ssem, rsem, device):
        pltpu.make_async_remote_copy(
            src_ref=src, dst_ref=dst, send_sem=ssem, recv_sem=rsem,
            device_id=device, device_id_type=MESH,
        ).start()

    def wait(sem, like):
        pltpu.make_async_copy(like, like, sem).wait()

    loads = [
        pltpu.make_async_copy(kd.at[0, pl.ds(mine, HALF)], acc, load_sem.at[0]),
        pltpu.make_async_copy(gd, gd_v, load_sem.at[1]),
        pltpu.make_async_copy(gm_hbm, gm_v, load_sem.at[2]),
        pltpu.make_async_copy(gp_hbm, gp_v, load_sem.at[3]),
        pltpu.make_async_copy(km_hbm, km, load_sem.at[4]),
        pltpu.make_async_copy(kp_hbm, kp, load_sem.at[5]),
    ]
    for cp in loads:
        cp.start()

    barrier = pltpu.get_barrier_semaphore()
    partners = plane + column
    for device in partners:
        pl.semaphore_signal(barrier, inc=1, device_id=device, device_id_type=MESH)
    pl.semaphore_wait(barrier, len(partners))

    for j in range(CHUNKS):
        send(
            kd.at[0, pl.ds(other + j * CROWS, CROWS)],
            r0.at[j], send_sem.at[0], sem0.at[j], sibling,
        )
    loads[1].wait()
    send(gd_v, g_core, gsend_sem.at[0], gc_sem, sibling)

    def block(j, o, q):
        return pl.multiple_of(j * CROWS + o * (CROWS // 2) + q * BROWS, 8)

    def cols(q):
        return pl.ds(pl.multiple_of(q * PCOLS, PCOLS), PCOLS)

    first = (x, y)
    second = (y, x)
    peers = ((xpeer, ypeer), (ypeer, xpeer))
    order = (1, 0, 2)

    loads[0].wait()
    for j in range(CHUNKS):
        wait(sem0.at[j], r0.at[j])
        rows = pl.ds(j * CROWS, CROWS)
        acc[rows] = acc[rows] + r0[j]
        for p in order:
            for o in range(2):
                q = (first[o] + p + 1) % 4
                send(
                    acc.at[pl.ds(block(j, o, q), BROWS)],
                    r1.at[j, o, p], send_sem.at[1], sem1.at[j, o], peers[o][0][p],
                )
        if j == 0:
            wait(gc_sem, g_core)
            g_x[x] = gd_v[...] + g_core[...]
            for p in range(3):
                send(g_x.at[x], g_x.at[x], gsend_sem.at[1], gx_sem, xpeer[p])
    wait(gx_sem, g_x.at[0:3])
    g_y[y] = (g_x[0] + g_x[1]) + (g_x[2] + g_x[3])
    for p in range(3):
        send(g_y.at[y], g_y.at[y], gsend_sem.at[2], gy_sem, ypeer[p])

    for j in range(CHUNKS):
        for o in range(2):
            wait(sem1.at[j, o], r1.at[j, o])
            rows = pl.ds(block(j, o, first[o]), BROWS)
            acc[rows] = (acc[rows] + r1[j, o, 0]) + (r1[j, o, 1] + r1[j, o, 2])
            for p in order:
                q = (second[o] + p + 1) % 4
                send(
                    acc.at[rows, cols(q)],
                    r2.at[j, o, p], send_sem.at[2], sem2.at[j, o], peers[o][1][p],
                )

    wait(gy_sem, g_y.at[0:3])
    for k in range(2, 6):
        loads[k].wait()
    g_avg = ((g_y[0] + g_y[1]) + (g_y[2] + g_y[3])) * (1.0 / NREP)
    g_mom = 0.9 * gm_v[...] + g_avg
    g_step = g_avg + 0.9 * g_mom
    gmn_out[...] = g_mom
    g_sq = g_step * g_step
    g_part = (g_sq[:, 0:128] + g_sq[:, 128:256]) + (g_sq[:, 256:384] + g_sq[:, 384:512])

    k_part = jnp.zeros((1, 128), jnp.float32)
    for j in range(CHUNKS):
        for o in range(2):
            wait(sem2.at[j, o], r2.at[j, o])
            own = cols(second[o])
            rows = pl.ds(block(j, o, first[o]), BROWS)
            piece = (acc[rows, own] + r2[j, o, 0]) + (r2[j, o, 1] + r2[j, o, 2])
            piece = piece * (1.0 / NREP)
            arows = pl.ds(mine + block(j, o, first[o]), BROWS)
            avg[arows, own] = piece
            for p in order:
                part = avg.at[arows, own]
                send(part, part, send_sem.at[3], sem3.at[j, o], peers[o][1][p])
            step = piece + 0.9 * (0.9 * km[arows, own] + piece)
            sq = step * step
            k_part = k_part + jnp.sum(sq[:, :128] + sq[:, 128:], axis=0, keepdims=True)

    row = lax.broadcasted_iota(jnp.int32, (8, 128), 0)
    own_z = z * CORES + c
    s_z[own_z] = jnp.where(row == 0, k_part, jnp.where(row == 1, g_part, 0.0))
    for device in column:
        send(s_z.at[own_z], s_z.at[own_z], ssend_sem.at[0], sz_sem, device)

    for j in range(CHUNKS):
        for o in range(2):
            wait(sem3.at[j, o], r2.at[j, o])
            part = avg.at[pl.ds(mine + block(j, o, first[o]), BROWS)]
            for p in order:
                send(part, part, send_sem.at[4], sem4.at[j, o], peers[o][0][p])

    wait(sz_sem, s_z.at[0:15])
    own_p = x * YS + y
    s_all = s_z[0]
    for k in range(1, ZS * CORES):
        s_all = s_all + s_z[k]
    s_p[own_p] = s_all
    for device in plane:
        send(s_p.at[own_p], s_p.at[own_p], ssend_sem.at[1], sp_sem, device)
    g_total = jnp.sum(s_all[1:2, :]) * 0.5
    g_scale = 0.7 / jnp.sqrt(jnp.full((1, 128), g_total, jnp.float32) / D + 1e-06)
    gn_out[...] = gp_v[...] - g_step * jnp.concatenate([g_scale] * 4, axis=1)

    def finish(base, rows):
        def step_rows(i, carry):
            at_rows = pl.ds(pl.multiple_of(base + i * 8, 8), 8)
            a = avg[at_rows]
            m = 0.9 * km[at_rows] + a
            mom[at_rows] = m
            stp[at_rows] = a + 0.9 * m
            return carry
        lax.fori_loop(0, rows // 8, step_rows, 0, unroll=2)

    for j in range(CHUNKS):
        for o in range(2):
            wait(sem4.at[j, o], r1.at[j, o])
        part = avg.at[pl.ds(mine + j * CROWS, CROWS)]
        send(part, part, send_sem.at[5], sem5.at[j], sibling)
        finish(mine + j * CROWS, CROWS)
    for j in range(CHUNKS):
        wait(sem5.at[j], r0.at[j])
        finish(other + j * CROWS, CROWS)

    wait(send_sem.at[0], r0)
    wait(send_sem.at[1], r1)
    wait(send_sem.at[2], r2)
    wait(send_sem.at[3], r2)
    wait(send_sem.at[4], r1)
    wait(send_sem.at[5], r0)
    wait(gsend_sem.at[0], g_core)
    wait(gsend_sem.at[1], g_x.at[0:3])
    wait(gsend_sem.at[2], g_y.at[0:3])
    wait(ssend_sem.at[0], s_z.at[0:15])
    wait(ssend_sem.at[1], s_p.at[0:15])
    wait(sp_sem, s_p.at[0:15])
    s_all = s_p[0]
    for k in range(1, XS * YS):
        s_all = s_all + s_p[k]
    k_total = jnp.sum(s_all[0:1, :])
    scale[...] = 0.7 / jnp.sqrt(jnp.full((8, 128), k_total, jnp.float32) / (D * KV) + 1e-06)


def tail_kernel(mom, stp, kp, scale, gn, gmn, kn_out, kmn_out, gn_out, gmn_out, kn, sem):
    copies = [
        pltpu.make_async_copy(mom, kmn_out, sem.at[0]),
        pltpu.make_async_copy(gn, gn_out, sem.at[1]),
        pltpu.make_async_copy(gmn, gmn_out, sem.at[2]),
    ]
    for cp in copies:
        cp.start()
    k_scale = jnp.concatenate([scale[...]] * (KV // 128), axis=1)
    size = ROWS // TAIL
    for t in range(TAIL):
        def step_rows(i, carry):
            rows = pl.ds(pl.multiple_of(t * size + i * 8, 8), 8)
            kn[rows] = kp[rows] - stp[rows] * k_scale
            return carry
        lax.fori_loop(0, size // 8, step_rows, 0, unroll=2)
        rows = pl.ds(t * size, size)
        cp = pltpu.make_async_copy(kn.at[rows], kn_out.at[rows], sem.at[3 + t])
        cp.start()
        copies.append(cp)
    for cp in copies:
        cp.wait()


def on_device(key_delta, gain_delta, key_params, key_moment, gain_params, gain_moment):
    f32 = jnp.float32
    dma = pltpu.SemaphoreType.DMA
    hbm = pl.BlockSpec(memory_space=pltpu.HBM)
    vmem = pl.BlockSpec(memory_space=pltpu.VMEM)
    gl = ROWS
    whole = jax.ShapeDtypeStruct((ROWS, KV), f32)
    line = jax.ShapeDtypeStruct((1, gl), f32)
    inputs = (
        key_delta, gain_delta, key_params, key_moment,
        gain_params.reshape(1, gl), gain_moment.reshape(1, gl),
    )
    inputs = tuple(pltpu.with_memory_space_constraint(a, pltpu.HBM) for a in inputs)
    parts = pl.pallas_call(
        comm_kernel,
        out_shape=(whole, whole, whole, jax.ShapeDtypeStruct((8, 128), f32), line, line),
        in_specs=[hbm] * 6,
        out_specs=[vmem] * 6,
        scratch_shapes=[
            pltpu.VMEM((HALF, KV), f32),
            pltpu.VMEM((CHUNKS, CROWS, KV), f32),
            pltpu.VMEM((CHUNKS, 2, 3, BROWS, KV), f32),
            pltpu.VMEM((CHUNKS, 2, 3, BROWS, PCOLS), f32),
            pltpu.VMEM((ROWS, KV), f32),
            pltpu.VMEM((ROWS, KV), f32),
            pltpu.VMEM((1, gl), f32),
            pltpu.VMEM((1, gl), f32),
            pltpu.VMEM((1, gl), f32),
            pltpu.VMEM((1, gl), f32),
            pltpu.VMEM((4, 1, gl), f32),
            pltpu.VMEM((4, 1, gl), f32),
            pltpu.VMEM((16, 8, 128), f32),
            pltpu.VMEM((16, 8, 128), f32),
            dma((6,)),
            dma((6,)),
            dma((CHUNKS,)),
            dma((CHUNKS, 2)),
            dma((CHUNKS, 2)),
            dma((CHUNKS, 2)),
            dma((CHUNKS, 2)),
            dma((CHUNKS,)),
            dma((3,)),
            dma,
            dma,
            dma,
            dma((2,)),
            dma,
            dma,
        ],
        compiler_params=pltpu.CompilerParams(
            collective_id=0, has_side_effects=True, vmem_limit_bytes=32 << 20
        ),
        name="worker_mean",
    )(*inputs)
    kn, kmn, gn, gmn = pl.pallas_call(
        tail_kernel,
        out_shape=(whole, whole, line, line),
        in_specs=[vmem] * 6,
        out_specs=[pl.BlockSpec(memory_space=pltpu.HBM)] * 4,
        scratch_shapes=[pltpu.VMEM((ROWS, KV), f32), dma((3 + TAIL,))],
        compiler_params=pltpu.CompilerParams(vmem_limit_bytes=32 << 20),
        name="apply_step",
    )(*parts)
    return kn, kmn, gn.reshape(gl), gmn.reshape(gl)


def solution(mesh):
    return jax.shard_map(
        on_device,
        mesh=mesh,
        in_specs=(
            P("replica", "fsdp", None),
            P("replica", "fsdp"),
            P("fsdp", None),
            P("fsdp", None),
            P("fsdp"),
            P("fsdp"),
        ),
        out_specs=(P("fsdp", None), P("fsdp", None), P("fsdp"), P("fsdp")),
        check_vma=False,
    )
```

```python
import jax
import jax.numpy as jnp
from jax import lax
from jax.experimental import pallas as pl
from jax.experimental.pallas import tpu as pltpu
from jax.sharding import PartitionSpec as P

D = 4096
KV = 1024
NREP = 32
SIDE, CORES, ZS = 4, 2, 8
ROWS = D // ZS
BR = ROWS // (CORES * 2 * 2 * SIDE)
SHAPE = (CORES, 2, 2, SIDE, BR, KV)
OWN = SHAPE[1:]
CUTS = [(True, 0, 8, 0, 512), (True, 0, 8, 512, 512), (True, 8, 8, 0, 512), (False, 8, 8, 512, 512)]
CHUNKS = len(CUTS)
EARLY = ZS // 2
MESH = pl.DeviceIdType.MESH


def comm_kernel(
    kd, gd, kp_hbm, km_hbm, gm_hbm,
    mom, stp, kp, total, gmn_out, gstep_out,
    acc, r0, r1a, r1b, r1, c2, r2, c3, avg, km,
    gd_v, gm_v, g_core, g_x, g_y, s_z, s_p,
    load_sem, send_sem, sem0, sem1a, sem1b, sem1, sem2, sem3, sem4, sem5,
    gsend_sem, gc_sem, gx_sem, gy_sem, ssend_sem, sz_sem, sp_sem, ready_sem, go_sem,
):
    r = lax.axis_index("replica")
    z = lax.axis_index("fsdp")
    x = r // (SIDE * CORES)
    y = (r // CORES) % SIDE
    c = r % CORES

    def at(px, py, pc):
        return ((px * SIDE + py) * CORES + pc, z)

    sibling = at(x, y, 1 - c)
    xpeer = [at((x + p) % SIDE, y, c) for p in (1, 2, 3)]
    ypeer = [at(x, (y + p) % SIDE, c) for p in (1, 2, 3)]
    away = (2, 1, 3, 0)
    plane = [at((x + p) % SIDE, (y + q) % SIDE, c) for p in away for q in away if p or q]
    column = [
        (at(x, y, (c + q) % 2)[0], (z + p) % ZS)
        for p in (4, 3, 5, 2, 6, 1, 7, 0) for q in (1, 0) if p or q
    ]
    barrier = pltpu.get_barrier_semaphore()

    def greet(sem, device):
        pl.semaphore_signal(sem, inc=1, device_id=device, device_id_type=MESH)

    def greet_column(sem, k):
        for q in range(CORES):
            greet(sem, (at(x, y, q)[0], k))

    early = z < EARLY
    for device in [sibling] + xpeer + ypeer:
        greet(barrier, device)
    for k in range(1, ZS):
        pl.when(jnp.logical_and(k > z, early))(lambda: greet_column(barrier, k))

    loads = [
        pltpu.make_async_copy(kd.at[c], acc, load_sem.at[0]),
        pltpu.make_async_copy(gd, gd_v, load_sem.at[1]),
        pltpu.make_async_copy(gm_hbm, gm_v, load_sem.at[2]),
        pltpu.make_async_copy(km_hbm, km, load_sem.at[3]),
        pltpu.make_async_copy(kp_hbm, kp, load_sem.at[4]),
    ]
    for cp in loads[:3]:
        cp.start()

    def send(src, dst, ssem, rsem, device):
        pltpu.make_async_remote_copy(
            src_ref=src, dst_ref=dst, send_sem=ssem, recv_sem=rsem,
            device_id=device, device_id_type=MESH,
        ).start()

    def wait(sem, like):
        pltpu.make_async_copy(like, like, sem).wait()

    pl.semaphore_wait(barrier, 1 + 2 * (SIDE - 1) + CORES * jnp.minimum(z, EARLY))

    def cut(j):
        _, a, n, b, w = CUTS[j]
        return pl.ds(a, n), pl.ds(b, w)

    def piece(j, q):
        _, a, n, b, w = CUTS[j]
        return pl.ds(a, n), pl.ds(pl.multiple_of(b + q * (w // SIDE), 128), w // SIDE)

    def part(j):
        _, a, n, b, w = CUTS[j]
        return pl.ds(a, n), pl.ds(b // SIDE, w // SIDE)

    for j in range(CHUNKS):
        R, C = cut(j)
        for o in range(2):
            send(
                kd.at[1 - c, o, :, :, R, C], r0.at[o, :, :, R, C],
                send_sem.at[0], sem0.at[j, o], sibling,
            )
    loads[1].wait()
    send(gd_v, g_core, gsend_sem.at[0], gc_sem, sibling)
    for cp in loads[3:]:
        cp.start()
    for k in range(EARLY):
        pl.when(k < z)(lambda: greet_column(ready_sem, k))

    first = (x, y)
    second = (y, x)
    far = (ypeer, xpeer)

    def on_axis(o, q):
        return at(q, y, c) if o == 0 else at(x, q, c)

    def pairing(o, u):
        i = first[o]
        swap, mirror = i + 1 - 2 * (i % 2), 3 - i
        loc = (i + 1) % SIDE if u == 0 else i
        near, last = (swap, mirror) if u == 0 else (mirror, swap)
        base = 2 * (loc // 2)
        return dict(
            near=on_axis(o, near), last=on_axis(o, last), loc=loc,
            group=base, sent=2 - base, mate=2 * base + 1 - loc,
        )

    both = [(o, u) for o in range(2) for u in range(2)]
    pair = {ou: pairing(*ou) for ou in both}
    axis = (xpeer, ypeer)
    paired = [j for j in range(CHUNKS) if CUTS[j][0]]

    def place(j, o, u):
        return pair[o, u]["loc"] if CUTS[j][0] else first[o]

    loads[0].wait()
    for j in range(CHUNKS):
        R, C = cut(j)
        for o in range(2):
            wait(sem0.at[j, o], r0.at[o, :, :, R, C])
            acc[o, :, :, R, C] = acc[o, :, :, R, C] + r0[o, :, :, R, C]
            if CUTS[j][0]:
                for u in range(2):
                    p = pair[o, u]
                    send(
                        acc.at[o, u, pl.ds(p["sent"], 2), R, C], r1a.at[o, u, :, R, C],
                        send_sem.at[1], sem1a.at[j, o, u], p["near"],
                    )
            else:
                for p in (1, 0, 2):
                    send(
                        acc.at[o, :, (first[o] + p + 1) % SIDE, R, C], r1.at[o, p, :, R, C],
                        send_sem.at[6], sem1.at[j, o], axis[o][p],
                    )
        if j == 0:
            wait(gc_sem, g_core)
            g_x[x] = gd_v[...] + g_core[...]
            for device in xpeer:
                send(g_x.at[x], g_x.at[x], gsend_sem.at[1], gx_sem, device)
    wait(gx_sem, g_x.at[0:3])
    g_y[y] = (g_x[0] + g_x[1]) + (g_x[2] + g_x[3])
    for device in ypeer:
        send(g_y.at[y], g_y.at[y], gsend_sem.at[2], gy_sem, device)

    for j in paired:
        R, C = cut(j)
        for o, u in both:
            p = pair[o, u]
            group = pl.ds(p["group"], 2)
            wait(sem1a.at[j, o, u], r1a.at[o, u, :, R, C])
            acc[o, u, group, R, C] = acc[o, u, group, R, C] + r1a[o, u, :, R, C]
            send(
                acc.at[o, u, p["mate"], R, C], r1b.at[o, u, R, C],
                send_sem.at[2], sem1b.at[j, o, u], p["last"],
            )
    for j in range(CHUNKS):
        R, C = cut(j)
        for o in range(2):
            if CUTS[j][0]:
                for u in range(2):
                    wait(sem1b.at[j, o, u], r1b.at[o, u, R, C])
                    c2[o, u, R, C] = acc[o, u, pair[o, u]["loc"], R, C] + r1b[o, u, R, C]
            else:
                wait(sem1.at[j, o], r1.at[o, :, :, R, C])
                c2[o, :, R, C] = (acc[o, :, first[o], R, C] + r1[o, 0, :, R, C]) + (r1[o, 1, :, R, C] + r1[o, 2, :, R, C])
            for p in (1, 0, 2):
                Rq, Cq = piece(j, (second[o] + p + 1) % SIDE)
                Rp, Cp = part(j)
                send(
                    c2.at[o, :, Rq, Cq], r2.at[o, p, :, Rp, Cp],
                    send_sem.at[3], sem2.at[j, o], far[o][p],
                )

    wait(gy_sem, g_y.at[0:3])
    for cp in loads[2:]:
        cp.wait()
    g_avg = ((g_y[0] + g_y[1]) + (g_y[2] + g_y[3])) * (1.0 / NREP)
    g_mom = 0.9 * gm_v[...] + g_avg
    g_step = g_avg + 0.9 * g_mom
    gmn_out[...] = g_mom
    gstep_out[...] = g_step
    g_sq = g_step * g_step
    g_part = (g_sq[:, 0:128] + g_sq[:, 128:256]) + (g_sq[:, 256:384] + g_sq[:, 384:512])

    @pl.when(early)
    def _():
        pl.semaphore_wait(ready_sem, CORES * (ZS - 1 - z))

    @pl.when(z == 0)
    def _():
        for k in range(EARLY, ZS):
            greet(go_sem, (r, k))

    k_part = jnp.zeros((8, 128), jnp.float32)
    for j in range(CHUNKS):
        Rp, Cp = part(j)
        for o in range(2):
            wait(sem2.at[j, o], r2.at[o, :, :, Rp, Cp])
            Rq, Cq = piece(j, second[o])
            mean = (c2[o, :, Rq, Cq] + r2[o, 0, :, Rp, Cp]) + (r2[o, 1, :, Rp, Cp] + r2[o, 2, :, Rp, Cp])
            mean = mean * (1.0 / NREP)
            c3[o, :, Rq, Cq] = mean
            for p in (1, 0, 2):
                send(
                    c3.at[o, :, Rq, Cq], c3.at[o, :, Rq, Cq],
                    send_sem.at[4], sem3.at[j, o], far[o][p],
                )
            for u in range(2):
                step = mean[u] + 0.9 * (0.9 * km[c, o, u, place(j, o, u), Rq, Cq] + mean[u])
                square = step * step
                for a in range(0, step.shape[0], 8):
                    for b in range(0, step.shape[1], 128):
                        k_part = k_part + square[a:a + 8, b:b + 128]

    @pl.when(jnp.logical_not(early))
    def _():
        pl.semaphore_wait(go_sem, 1)

    own_z = z * CORES + c
    s_z[own_z, :, 0:128] = jnp.sum(k_part, axis=0, keepdims=True)
    s_z[own_z, :, 128:256] = g_part
    for device in column:
        send(s_z.at[own_z], s_z.at[own_z], ssend_sem.at[0], sz_sem, device)

    for j in range(CHUNKS):
        R, C = cut(j)
        for o in range(2):
            wait(sem3.at[j, o], r2.at[o, :, :, part(j)[0], part(j)[1]])
            for u in range(2):
                avg[c, o, u, place(j, o, u), R, C] = c3[o, u, R, C]
            for p in (1, 0, 2):
                for u in range(2):
                    send(
                        c3.at[o, u, R, C], avg.at[c, o, u, place(j, o, u), R, C],
                        send_sem.at[5], sem4.at[j, o], axis[o][p],
                    )

    def plane_round():
        wait(sz_sem, s_z.at[0:15])
        s_all = s_z[0]
        for k in range(1, ZS * CORES):
            s_all = s_all + s_z[k]
        own_p = x * SIDE + y
        s_p[own_p] = s_all[:, 0:128]
        total[:, 128:256] = s_all[:, 128:256]
        for device in plane:
            send(s_p.at[own_p], s_p.at[own_p], ssend_sem.at[1], sp_sem, device)

    def finish(side, o, j):
        R, C = cut(j)

        def block(i, carry):
            at_block = (side, o, i // SIDE, i % SIDE, R, C)
            a = avg[at_block]
            m = 0.9 * km[at_block] + a
            mom[at_block] = m
            stp[at_block] = a + 0.9 * m
            return carry
        lax.fori_loop(0, 2 * SIDE, block, 0, unroll=2)

    plane_round()
    for j in range(CHUNKS):
        R, C = cut(j)
        for o in range(2):
            wait(sem4.at[j, o], r1.at[o, :, :, R, C])
            blocks = avg.at[c, o, :, :, R, C]
            send(blocks, blocks, send_sem.at[7], sem5.at[j, o], sibling)
    for j in range(CHUNKS):
        for o in range(2):
            finish(c, o, j)
    for j in range(CHUNKS):
        R, C = cut(j)
        for o in range(2):
            wait(sem5.at[j, o], r0.at[o, :, :, R, C])
            finish(1 - c, o, j)

    def sent(sem, refs):
        for ref in refs:
            wait(sem, ref)

    straight = [j for j in range(CHUNKS) if not CUTS[j][0]]
    sent(send_sem.at[1], [r1a.at[:, :, :, cut(j)[0], cut(j)[1]] for j in paired])
    sent(send_sem.at[2], [r1b.at[:, :, cut(j)[0], cut(j)[1]] for j in paired])
    sent(send_sem.at[6], [r1.at[:, :, :, cut(j)[0], cut(j)[1]] for j in straight])
    wait(send_sem.at[5], r1)
    wait(send_sem.at[0], r0)
    wait(send_sem.at[3], r2)
    wait(send_sem.at[4], r2)
    wait(send_sem.at[7], r0)
    wait(gsend_sem.at[0], g_core)
    wait(gsend_sem.at[1], g_x.at[0:3])
    wait(gsend_sem.at[2], g_y.at[0:3])
    wait(ssend_sem.at[0], s_z.at[0:15])
    wait(ssend_sem.at[1], s_p.at[0:15])
    wait(sp_sem, s_p.at[0:15])
    s_all = s_p[0]
    for k in range(1, SIDE * SIDE):
        s_all = s_all + s_p[k]
    total[:, 0:128] = s_all


def tail_kernel(
    mom, stp, kp, total, gmn, g_step, gp_hbm, kn_out, kmn_out, gn_out, gmn_out, kn, gn, gp, sem
):
    load = pltpu.make_async_copy(gp_hbm, gp, sem.at[0])
    load.start()
    copies = [
        pltpu.make_async_copy(mom, kmn_out, sem.at[1]),
        pltpu.make_async_copy(gmn, gmn_out, sem.at[2]),
    ]
    for cp in copies:
        cp.start()
    k_sum = jnp.full((8, 128), jnp.sum(total[:, 0:128]), jnp.float32)
    k_scale = 0.7 / jnp.sqrt(k_sum / (D * KV) + 1e-06)
    k_scale = jnp.concatenate([k_scale] * (KV // 128), axis=1)
    k_scale = jnp.concatenate([k_scale] * (BR // 8), axis=0)
    for t in range(CORES * 2 * 2):
        blocks = (t // 4, t // 2 % 2, t % 2)

        def block(i, carry):
            kn[blocks + (i,)] = kp[blocks + (i,)] - stp[blocks + (i,)] * k_scale
            return carry
        lax.fori_loop(0, SIDE, block, 0)
        cp = pltpu.make_async_copy(kn.at[blocks], kn_out.at[blocks], sem.at[4 + t])
        cp.start()
        copies.append(cp)
    load.wait()
    g_sum = jnp.full((1, ROWS), jnp.sum(total[:, 128:256]) * (1.0 / CORES), jnp.float32)
    gn[...] = gp[...] - g_step[...] * (0.7 / jnp.sqrt(g_sum / D + 1e-06))
    cp = pltpu.make_async_copy(gn, gn_out, sem.at[3])
    cp.start()
    copies.append(cp)
    for cp in copies:
        cp.wait()


def on_device(key_delta, gain_delta, key_params, key_moment, gain_params, gain_moment):
    f32 = jnp.float32
    dma = pltpu.SemaphoreType.DMA
    signal = pltpu.SemaphoreType.REGULAR
    vector = pltpu.VMEM
    hbm = pl.BlockSpec(memory_space=pltpu.HBM)
    vmem = pl.BlockSpec(memory_space=pltpu.VMEM)
    whole = jax.ShapeDtypeStruct(SHAPE, f32)
    line = jax.ShapeDtypeStruct((1, ROWS), f32)
    hold = lambda a: pltpu.with_memory_space_constraint(a, pltpu.HBM)
    rows = lambda a: a.reshape(SHAPE)
    inputs = (rows(key_delta), gain_delta, rows(key_params), rows(key_moment), gain_moment.reshape(1, ROWS))
    parts = pl.pallas_call(
        comm_kernel,
        out_shape=(whole, whole, whole, jax.ShapeDtypeStruct((1, 256), f32), line, line),
        in_specs=[hbm] * 5,
        out_specs=[vmem] * 6,
        scratch_shapes=[
            vector(OWN, f32),
            vector(OWN, f32),
            vector((2, 2, 2, BR, KV), f32),
            vector((2, 2, BR, KV), f32),
            vector((2, 3, 2, BR, KV), f32),
            vector((2, 2, BR, KV), f32),
            vector((2, 3, 2, BR, KV // SIDE), f32),
            vector((2, 2, BR, KV), f32),
            vector(SHAPE, f32),
            vector(SHAPE, f32),
            vector((1, ROWS), f32),
            vector((1, ROWS), f32),
            vector((1, ROWS), f32),
            vector((4, 1, ROWS), f32),
            vector((4, 1, ROWS), f32),
            vector((16, 1, 256), f32),
            vector((16, 1, 128), f32),
            dma((5,)),
            dma((8,)),
            dma((CHUNKS, 2)),
            dma((CHUNKS, 2, 2)),
            dma((CHUNKS, 2, 2)),
            dma((CHUNKS, 2)),
            dma((CHUNKS, 2)),
            dma((CHUNKS, 2)),
            dma((CHUNKS, 2)),
            dma((CHUNKS, 2)),
            dma((3,)),
            dma,
            dma,
            dma,
            dma((2,)),
            dma,
            dma,
            signal,
            signal,
        ],
        compiler_params=pltpu.CompilerParams(
            collective_id=0, has_side_effects=True, vmem_limit_bytes=32 << 20
        ),
        name="worker_mean",
    )(*map(hold, inputs))
    kn, kmn, gn, gmn = pl.pallas_call(
        tail_kernel,
        out_shape=(whole, whole, line, line),
        in_specs=[vmem] * 6 + [hbm],
        out_specs=[hbm] * 4,
        scratch_shapes=[
            vector(SHAPE, f32),
            vector((1, ROWS), f32),
            vector((1, ROWS), f32),
            dma((4 + CORES * 2 * 2,)),
        ],
        compiler_params=pltpu.CompilerParams(vmem_limit_bytes=32 << 20),
        name="apply_step",
    )(*parts, hold(gain_params.reshape(1, ROWS)))
    return kn.reshape(ROWS, KV), kmn.reshape(ROWS, KV), gn.reshape(ROWS), gmn.reshape(ROWS)


def solution(mesh):
    return jax.shard_map(
        on_device,
        mesh=mesh,
        in_specs=(
            P("replica", "fsdp", None),
            P("replica", "fsdp"),
            P("fsdp", None),
            P("fsdp", None),
            P("fsdp"),
            P("fsdp"),
        ),
        out_specs=(P("fsdp", None), P("fsdp", None), P("fsdp"), P("fsdp")),
        check_vma=False,
    )
```

```python
import jax
import jax.numpy as jnp
from jax import lax
from jax.experimental import pallas as pl
from jax.experimental.pallas import tpu as pltpu
from jax.sharding import PartitionSpec as P

D = 4096
KV = 1024
NREP = 32
SIDE, CORES, ZS = 4, 2, 8
ROWS = D // ZS
BR = ROWS // (CORES * 2 * 2 * SIDE)
SHAPE = (CORES, 2, 2, SIDE, BR, KV)
OWN = SHAPE[1:]
CUTS = [(True, 0, 8, 0, 512), (True, 0, 8, 512, 512), (True, 8, 8, 0, 512), (False, 8, 8, 512, 512)]
CHUNKS = len(CUTS)
EARLY = ZS // 2
DIRECT = (1,)
MESH = pl.DeviceIdType.MESH


def comm_kernel(
    kd, gd, kp_hbm, km_hbm, gm_hbm,
    mom, stp, kp, total, gmn_out, gstep_out,
    acc, r0, r1a, r1b, r1, c2, r2, c3, avg, km,
    gd_v, gm_v, g_core, g_x, g_y, s_z, s_p, s_d,
    load_sem, send_sem, sem0, sem1a, sem1b, sem1, sem2, sem3, sem4, sem5,
    gsend_sem, gc_sem, gx_sem, gy_sem, ssend_sem, sz_sem, sp_sem, sd_sem, ready_sem, go_sem,
):
    r = lax.axis_index("replica")
    z = lax.axis_index("fsdp")
    x = r // (SIDE * CORES)
    y = (r // CORES) % SIDE
    c = r % CORES

    def at(px, py, pc):
        return ((px * SIDE + py) * CORES + pc, z)

    sibling = at(x, y, 1 - c)
    xpeer = [at((x + p) % SIDE, y, c) for p in (1, 2, 3)]
    ypeer = [at(x, (y + p) % SIDE, c) for p in (1, 2, 3)]
    away = (2, 1, 3, 0)
    plane = [at((x + p) % SIDE, (y + q) % SIDE, c) for p in away for q in away if p or q]
    column = [
        (at(x, y, (c + q) % 2)[0], (z + p) % ZS)
        for p in (4, 3, 5, 2, 6, 1, 7, 0) for q in (1, 0) if p or q
    ]
    barrier = pltpu.get_barrier_semaphore()

    def greet(sem, device):
        pl.semaphore_signal(sem, inc=1, device_id=device, device_id_type=MESH)

    def greet_column(sem, k):
        for q in range(CORES):
            greet(sem, (at(x, y, q)[0], k))

    early = z < EARLY
    for device in [sibling] + xpeer + ypeer:
        greet(barrier, device)
    for k in range(1, ZS):
        pl.when(jnp.logical_and(k > z, early))(lambda: greet_column(barrier, k))

    loads = [
        pltpu.make_async_copy(kd.at[c], acc, load_sem.at[0]),
        pltpu.make_async_copy(gd, gd_v, load_sem.at[1]),
        pltpu.make_async_copy(gm_hbm, gm_v, load_sem.at[2]),
        pltpu.make_async_copy(km_hbm, km, load_sem.at[3]),
        pltpu.make_async_copy(kp_hbm, kp, load_sem.at[4]),
    ]
    for cp in loads[:3]:
        cp.start()

    def send(src, dst, ssem, rsem, device):
        pltpu.make_async_remote_copy(
            src_ref=src, dst_ref=dst, send_sem=ssem, recv_sem=rsem,
            device_id=device, device_id_type=MESH,
        ).start()

    def wait(sem, like):
        pltpu.make_async_copy(like, like, sem).wait()

    pl.semaphore_wait(barrier, 1 + 2 * (SIDE - 1) + CORES * jnp.minimum(z, EARLY))

    def cut(j):
        _, a, n, b, w = CUTS[j]
        return pl.ds(a, n), pl.ds(b, w)

    def piece(j, q):
        _, a, n, b, w = CUTS[j]
        return pl.ds(a, n), pl.ds(pl.multiple_of(b + q * (w // SIDE), 128), w // SIDE)

    def part(j):
        _, a, n, b, w = CUTS[j]
        return pl.ds(a, n), pl.ds(b // SIDE, w // SIDE)

    for j in range(CHUNKS):
        R, C = cut(j)
        for o in range(2):
            send(
                kd.at[1 - c, o, :, :, R, C], r0.at[o, :, :, R, C],
                send_sem.at[0], sem0.at[j, o], sibling,
            )
    loads[1].wait()
    send(gd_v, g_core, gsend_sem.at[0], gc_sem, sibling)
    for cp in loads[3:]:
        cp.start()
    for k in range(EARLY):
        pl.when(k < z)(lambda: greet_column(ready_sem, k))

    first = (x, y)
    second = (y, x)
    far = (ypeer, xpeer)

    def on_axis(o, q):
        return at(q, y, c) if o == 0 else at(x, q, c)

    def pairing(o, u):
        i = first[o]
        swap, mirror = i + 1 - 2 * (i % 2), 3 - i
        loc = (i + 1) % SIDE if u == 0 else i
        near, last = (swap, mirror) if u == 0 else (mirror, swap)
        base = 2 * (loc // 2)
        return dict(
            near=on_axis(o, near), last=on_axis(o, last), loc=loc,
            group=base, sent=2 - base, mate=2 * base + 1 - loc,
        )

    both = [(o, u) for o in range(2) for u in range(2)]
    pair = {ou: pairing(*ou) for ou in both}
    axis = (xpeer, ypeer)
    paired = [j for j in range(CHUNKS) if CUTS[j][0]]

    def place(j, o, u):
        return pair[o, u]["loc"] if CUTS[j][0] else first[o]

    loads[0].wait()
    for j in range(CHUNKS):
        R, C = cut(j)
        for o in range(2):
            wait(sem0.at[j, o], r0.at[o, :, :, R, C])
            acc[o, :, :, R, C] = acc[o, :, :, R, C] + r0[o, :, :, R, C]
            if CUTS[j][0]:
                for u in range(2):
                    p = pair[o, u]
                    send(
                        acc.at[o, u, pl.ds(p["sent"], 2), R, C], r1a.at[o, u, :, R, C],
                        send_sem.at[1], sem1a.at[j, o, u], p["near"],
                    )
            else:
                for p in (1, 0, 2):
                    send(
                        acc.at[o, :, (first[o] + p + 1) % SIDE, R, C], r1.at[o, p, :, R, C],
                        send_sem.at[6], sem1.at[j, o], axis[o][p],
                    )
        if j == 0:
            wait(gc_sem, g_core)
            g_x[x] = gd_v[...] + g_core[...]
            for device in xpeer:
                send(g_x.at[x], g_x.at[x], gsend_sem.at[1], gx_sem, device)
    wait(gx_sem, g_x.at[0:3])
    g_y[y] = (g_x[0] + g_x[1]) + (g_x[2] + g_x[3])
    for device in ypeer:
        send(g_y.at[y], g_y.at[y], gsend_sem.at[2], gy_sem, device)

    for j in paired:
        R, C = cut(j)
        for o, u in both:
            p = pair[o, u]
            group = pl.ds(p["group"], 2)
            wait(sem1a.at[j, o, u], r1a.at[o, u, :, R, C])
            acc[o, u, group, R, C] = acc[o, u, group, R, C] + r1a[o, u, :, R, C]
            send(
                acc.at[o, u, p["mate"], R, C], r1b.at[o, u, R, C],
                send_sem.at[2], sem1b.at[j, o, u], p["last"],
            )
    for j in range(CHUNKS):
        R, C = cut(j)
        for o in range(2):
            if CUTS[j][0]:
                for u in range(2):
                    wait(sem1b.at[j, o, u], r1b.at[o, u, R, C])
                    c2[o, u, R, C] = acc[o, u, pair[o, u]["loc"], R, C] + r1b[o, u, R, C]
            else:
                wait(sem1.at[j, o], r1.at[o, :, :, R, C])
                c2[o, :, R, C] = (acc[o, :, first[o], R, C] + r1[o, 0, :, R, C]) + (r1[o, 1, :, R, C] + r1[o, 2, :, R, C])
            for p in (1, 0, 2):
                Rq, Cq = piece(j, (second[o] + p + 1) % SIDE)
                Rp, Cp = part(j)
                send(
                    c2.at[o, :, Rq, Cq], r2.at[o, p, :, Rp, Cp],
                    send_sem.at[3], sem2.at[j, o], far[o][p],
                )

    wait(gy_sem, g_y.at[0:3])
    for cp in loads[2:]:
        cp.wait()
    g_avg = ((g_y[0] + g_y[1]) + (g_y[2] + g_y[3])) * (1.0 / NREP)
    g_mom = 0.9 * gm_v[...] + g_avg
    g_step = g_avg + 0.9 * g_mom
    gmn_out[...] = g_mom
    gstep_out[...] = g_step
    g_sq = g_step * g_step
    g_part = (g_sq[:, 0:128] + g_sq[:, 128:256]) + (g_sq[:, 256:384] + g_sq[:, 384:512])

    @pl.when(early)
    def _():
        pl.semaphore_wait(ready_sem, CORES * (ZS - 1 - z))

    k_part = jnp.zeros((8, 128), jnp.float32)
    for j in range(CHUNKS):
        Rp, Cp = part(j)
        for o in range(2):
            wait(sem2.at[j, o], r2.at[o, :, :, Rp, Cp])
            Rq, Cq = piece(j, second[o])
            mean = (c2[o, :, Rq, Cq] + r2[o, 0, :, Rp, Cp]) + (r2[o, 1, :, Rp, Cp] + r2[o, 2, :, Rp, Cp])
            mean = mean * (1.0 / NREP)
            c3[o, :, Rq, Cq] = mean
            for p in (1, 0, 2):
                send(
                    c3.at[o, :, Rq, Cq], c3.at[o, :, Rq, Cq],
                    send_sem.at[4], sem3.at[j, o], far[o][p],
                )
            for u in range(2):
                step = mean[u] + 0.9 * (0.9 * km[c, o, u, place(j, o, u), Rq, Cq] + mean[u])
                square = step * step
                for a in range(0, step.shape[0], 8):
                    for b in range(0, step.shape[1], 128):
                        k_part = k_part + square[a:a + 8, b:b + 128]
        if j == 0:
            @pl.when(z == 0)
            def _():
                for k in range(1, ZS):
                    greet(go_sem, (r, k))

    @pl.when(z > 0)
    def _():
        pl.semaphore_wait(go_sem, 1)

    own_z = z * CORES + c
    own_p = x * SIDE + y
    own_d = own_z * SIDE * SIDE + own_p
    k_line = jnp.sum(k_part, axis=0, keepdims=True)
    s_z[own_z, :, 0:128] = k_line
    s_z[own_z, :, 128:256] = g_part
    at_zero = [jnp.logical_and(z == 0, r == d) for d in DIRECT]
    direct = at_zero[0]
    for here in at_zero[1:]:
        direct = jnp.logical_or(direct, here)
    for d, here in zip(DIRECT, at_zero):
        @pl.when(jnp.logical_not(here))
        def _():
            send(s_z.at[own_z, :, pl.ds(0, 128)], s_d.at[own_d], ssend_sem.at[2], sd_sem, (d, 0))

    @pl.when(direct)
    def _():
        s_d[own_d] = k_line

    for device in column:
        send(s_z.at[own_z], s_z.at[own_z], ssend_sem.at[0], sz_sem, device)

    for j in range(CHUNKS):
        R, C = cut(j)
        for o in range(2):
            wait(sem3.at[j, o], r2.at[o, :, :, part(j)[0], part(j)[1]])
            for u in range(2):
                avg[c, o, u, place(j, o, u), R, C] = c3[o, u, R, C]
            for p in (1, 0, 2):
                for u in range(2):
                    send(
                        c3.at[o, u, R, C], avg.at[c, o, u, place(j, o, u), R, C],
                        send_sem.at[5], sem4.at[j, o], axis[o][p],
                    )

    def plane_round():
        wait(sz_sem, s_z.at[0:15])
        s_all = s_z[0]
        for k in range(1, ZS * CORES):
            s_all = s_all + s_z[k]
        s_p[own_p] = s_all[:, 0:128]
        total[:, 128:256] = s_all[:, 128:256]
        for device in plane:
            skip = device[0] == DIRECT[0]
            for d in DIRECT[1:]:
                skip = jnp.logical_or(skip, device[0] == d)

            @pl.when(jnp.logical_not(jnp.logical_and(z == 0, skip)))
            def _():
                send(s_p.at[own_p], s_p.at[own_p], ssend_sem.at[1], sp_sem, device)

    def finish(side, o, j):
        R, C = cut(j)

        def block(i, carry):
            at_block = (side, o, i // SIDE, i % SIDE, R, C)
            a = avg[at_block]
            m = 0.9 * km[at_block] + a
            mom[at_block] = m
            stp[at_block] = a + 0.9 * m
            return carry
        lax.fori_loop(0, 2 * SIDE, block, 0, unroll=2)

    plane_round()
    for j in range(CHUNKS):
        R, C = cut(j)
        for o in range(2):
            wait(sem4.at[j, o], r1.at[o, :, :, R, C])
            blocks = avg.at[c, o, :, :, R, C]
            send(blocks, blocks, send_sem.at[7], sem5.at[j, o], sibling)
    for j in range(CHUNKS):
        for o in range(2):
            finish(c, o, j)
    for j in range(CHUNKS):
        R, C = cut(j)
        for o in range(2):
            wait(sem5.at[j, o], r0.at[o, :, :, R, C])
            finish(1 - c, o, j)

    def sent(sem, refs):
        for ref in refs:
            wait(sem, ref)

    straight = [j for j in range(CHUNKS) if not CUTS[j][0]]
    sent(send_sem.at[1], [r1a.at[:, :, :, cut(j)[0], cut(j)[1]] for j in paired])
    sent(send_sem.at[2], [r1b.at[:, :, cut(j)[0], cut(j)[1]] for j in paired])
    sent(send_sem.at[6], [r1.at[:, :, :, cut(j)[0], cut(j)[1]] for j in straight])
    wait(send_sem.at[5], r1)
    wait(send_sem.at[0], r0)
    wait(send_sem.at[3], r2)
    wait(send_sem.at[4], r2)
    wait(send_sem.at[7], r0)
    wait(gsend_sem.at[0], g_core)
    wait(gsend_sem.at[1], g_x.at[0:3])
    wait(gsend_sem.at[2], g_y.at[0:3])
    wait(ssend_sem.at[0], s_z.at[0:15])
    wait(ssend_sem.at[1], s_p.at[0:15 - len(DIRECT)])
    for d, here in zip(DIRECT, at_zero):
        skipped = jnp.logical_and(z == 0, jnp.logical_and(c == d % CORES, jnp.logical_not(here)))

        @pl.when(jnp.logical_not(skipped))
        def _():
            wait(ssend_sem.at[1], s_p.at[0])

        @pl.when(jnp.logical_not(here))
        def _():
            wait(ssend_sem.at[2], s_d.at[0])

    @pl.when(jnp.logical_not(direct))
    def _():
        wait(sp_sem, s_p.at[0:15])
        s_all = s_p[0]
        for k in range(1, SIDE * SIDE):
            s_all = s_all + s_p[k]
        total[:, 0:128] = s_all

    @pl.when(direct)
    def _():
        wait(sd_sem, s_d.at[0:255])
        column_sums = s_d[0:16]
        for k in range(1, ZS * CORES):
            column_sums = column_sums + s_d[16 * k:16 * k + 16]
        s_all = column_sums[0]
        for k in range(1, SIDE * SIDE):
            s_all = s_all + column_sums[k]
        total[:, 0:128] = s_all


def tail_kernel(
    mom, stp, kp, total, gmn, g_step, gp_hbm, kn_out, kmn_out, gn_out, gmn_out, kn, gn, gp, sem
):
    load = pltpu.make_async_copy(gp_hbm, gp, sem.at[0])
    load.start()
    copies = [
        pltpu.make_async_copy(mom, kmn_out, sem.at[1]),
        pltpu.make_async_copy(gmn, gmn_out, sem.at[2]),
    ]
    for cp in copies:
        cp.start()
    k_sum = jnp.full((8, 128), jnp.sum(total[:, 0:128]), jnp.float32)
    k_scale = 0.7 / jnp.sqrt(k_sum / (D * KV) + 1e-06)
    k_scale = jnp.concatenate([k_scale] * (KV // 128), axis=1)
    k_scale = jnp.concatenate([k_scale] * (BR // 8), axis=0)
    for t in range(CORES * 2 * 2):
        blocks = (t // 4, t // 2 % 2, t % 2)

        def block(i, carry):
            kn[blocks + (i,)] = kp[blocks + (i,)] - stp[blocks + (i,)] * k_scale
            return carry
        lax.fori_loop(0, SIDE, block, 0)
        cp = pltpu.make_async_copy(kn.at[blocks], kn_out.at[blocks], sem.at[4 + t])
        cp.start()
        copies.append(cp)
    load.wait()
    g_sum = jnp.full((1, ROWS), jnp.sum(total[:, 128:256]) * (1.0 / CORES), jnp.float32)
    gn[...] = gp[...] - g_step[...] * (0.7 / jnp.sqrt(g_sum / D + 1e-06))
    cp = pltpu.make_async_copy(gn, gn_out, sem.at[3])
    cp.start()
    copies.append(cp)
    for cp in copies:
        cp.wait()


def on_device(key_delta, gain_delta, key_params, key_moment, gain_params, gain_moment):
    f32 = jnp.float32
    dma = pltpu.SemaphoreType.DMA
    signal = pltpu.SemaphoreType.REGULAR
    vector = pltpu.VMEM
    hbm = pl.BlockSpec(memory_space=pltpu.HBM)
    vmem = pl.BlockSpec(memory_space=pltpu.VMEM)
    whole = jax.ShapeDtypeStruct(SHAPE, f32)
    line = jax.ShapeDtypeStruct((1, ROWS), f32)
    hold = lambda a: pltpu.with_memory_space_constraint(a, pltpu.HBM)
    rows = lambda a: a.reshape(SHAPE)
    inputs = (rows(key_delta), gain_delta, rows(key_params), rows(key_moment), gain_moment.reshape(1, ROWS))
    parts = pl.pallas_call(
        comm_kernel,
        out_shape=(whole, whole, whole, jax.ShapeDtypeStruct((1, 256), f32), line, line),
        in_specs=[hbm] * 5,
        out_specs=[vmem] * 6,
        scratch_shapes=[
            vector(OWN, f32),
            vector(OWN, f32),
            vector((2, 2, 2, BR, KV), f32),
            vector((2, 2, BR, KV), f32),
            vector((2, 3, 2, BR, KV), f32),
            vector((2, 2, BR, KV), f32),
            vector((2, 3, 2, BR, KV // SIDE), f32),
            vector((2, 2, BR, KV), f32),
            vector(SHAPE, f32),
            vector(SHAPE, f32),
            vector((1, ROWS), f32),
            vector((1, ROWS), f32),
            vector((1, ROWS), f32),
            vector((4, 1, ROWS), f32),
            vector((4, 1, ROWS), f32),
            vector((16, 1, 256), f32),
            vector((16, 1, 128), f32),
            vector((256, 1, 128), f32),
            dma((5,)),
            dma((8,)),
            dma((CHUNKS, 2)),
            dma((CHUNKS, 2, 2)),
            dma((CHUNKS, 2, 2)),
            dma((CHUNKS, 2)),
            dma((CHUNKS, 2)),
            dma((CHUNKS, 2)),
            dma((CHUNKS, 2)),
            dma((CHUNKS, 2)),
            dma((3,)),
            dma,
            dma,
            dma,
            dma((3,)),
            dma,
            dma,
            dma,
            signal,
            signal,
        ],
        compiler_params=pltpu.CompilerParams(
            collective_id=0, has_side_effects=True, vmem_limit_bytes=32 << 20
        ),
        name="worker_mean",
    )(*map(hold, inputs))
    kn, kmn, gn, gmn = pl.pallas_call(
        tail_kernel,
        out_shape=(whole, whole, line, line),
        in_specs=[vmem] * 6 + [hbm],
        out_specs=[hbm] * 4,
        scratch_shapes=[
            vector(SHAPE, f32),
            vector((1, ROWS), f32),
            vector((1, ROWS), f32),
            dma((4 + CORES * 2 * 2,)),
        ],
        compiler_params=pltpu.CompilerParams(vmem_limit_bytes=32 << 20),
        name="apply_step",
    )(*parts, hold(gain_params.reshape(1, ROWS)))
    return kn.reshape(ROWS, KV), kmn.reshape(ROWS, KV), gn.reshape(ROWS), gmn.reshape(ROWS)


def solution(mesh):
    return jax.shard_map(
        on_device,
        mesh=mesh,
        in_specs=(
            P("replica", "fsdp", None),
            P("replica", "fsdp"),
            P("fsdp", None),
            P("fsdp", None),
            P("fsdp"),
            P("fsdp"),
        ),
        out_specs=(P("fsdp", None), P("fsdp", None), P("fsdp"), P("fsdp")),
        check_vma=False,
    )
```

```python
import jax
import jax.numpy as jnp
from jax import lax
from jax.experimental import pallas as pl
from jax.experimental.pallas import tpu as pltpu
from jax.sharding import PartitionSpec as P

D = 4096
KV = 1024
NREP = 32
SIDE, CORES, ZS = 4, 2, 8
ROWS = D // ZS
BR = ROWS // (CORES * 2 * 2 * SIDE)
SHAPE = (CORES, 2, 2, SIDE, BR, KV)
OWN = SHAPE[1:]
CUTS = [(True, 0, 8, 0, 512), (True, 0, 8, 512, 512), (True, 8, 8, 0, 512), (False, 8, 8, 512, 512)]
CHUNKS = len(CUTS)
EARLY = 1
SLACK = 1
DIRECT = (1, 2, 8)
MESH = pl.DeviceIdType.MESH


def comm_kernel(
    kd, gd, kp_hbm, km_hbm, gm_hbm,
    mom, stp, kp, total, gmn_out, gstep_out,
    acc, r0, r1a, r1b, r1, c2, r2, c3, avg, km,
    gd_v, gm_v, g_core, g_x, g_y, s_z, s_p, s_d,
    load_sem, send_sem, sem0, sem1a, sem1b, sem1, sem2, sem3, sem4, sem5,
    gsend_sem, gc_sem, gx_sem, gy_sem, ssend_sem, sz_sem, sp_sem, sd_sem, ready_sem, go_sem, pair_sem,
):
    r = lax.axis_index("replica")
    z = lax.axis_index("fsdp")
    x = r // (SIDE * CORES)
    y = (r // CORES) % SIDE
    c = r % CORES

    def at(px, py, pc):
        return ((px * SIDE + py) * CORES + pc, z)

    sibling = at(x, y, 1 - c)
    xpeer = [at((x + p) % SIDE, y, c) for p in (1, 2, 3)]
    ypeer = [at(x, (y + p) % SIDE, c) for p in (1, 2, 3)]
    away = (2, 1, 3, 0)
    plane = [at((x + p) % SIDE, (y + q) % SIDE, c) for p in away for q in away if p or q]
    column = [
        (at(x, y, (c + q) % 2)[0], (z + p) % ZS)
        for p in (4, 3, 5, 2, 6, 1, 7, 0) for q in (1, 0) if p or q
    ]
    barrier = pltpu.get_barrier_semaphore()

    def greet(sem, device):
        pl.semaphore_signal(sem, inc=1, device_id=device, device_id_type=MESH)

    def greet_column(sem, k):
        for q in range(CORES):
            greet(sem, (at(x, y, q)[0], k))

    early = z < EARLY
    for p in (2, 1, 3):
        greet(barrier, at((x + p) % SIDE, y, 0))
        greet(barrier, at(x, (y + p) % SIDE, 0))
    pl.when(c == 0)(lambda: greet(barrier, sibling))
    for k in range(1, ZS):
        pl.when(jnp.logical_and(k > z, early))(lambda: greet_column(barrier, k))

    loads = [
        pltpu.make_async_copy(kd.at[c], acc, load_sem.at[0]),
        pltpu.make_async_copy(gd, gd_v, load_sem.at[1]),
        pltpu.make_async_copy(gm_hbm, gm_v, load_sem.at[2]),
        pltpu.make_async_copy(km_hbm, km, load_sem.at[3]),
        pltpu.make_async_copy(kp_hbm, kp, load_sem.at[4]),
    ]
    for cp in loads[:3]:
        cp.start()

    def send(src, dst, ssem, rsem, device):
        pltpu.make_async_remote_copy(
            src_ref=src, dst_ref=dst, send_sem=ssem, recv_sem=rsem,
            device_id=device, device_id_type=MESH,
        ).start()

    def wait(sem, like):
        pltpu.make_async_copy(like, like, sem).wait()

    lower = CORES * jnp.minimum(z, EARLY)

    @pl.when(c == 1)
    def _():
        pl.semaphore_wait(barrier, 1 + lower)
        greet(pair_sem, sibling)

    @pl.when(c == 0)
    def _():
        pl.semaphore_wait(pair_sem, 1)

    for k in range(EARLY):
        pl.when(k < z)(lambda: greet_column(ready_sem, k))

    def cut(j):
        _, a, n, b, w = CUTS[j]
        return pl.ds(a, n), pl.ds(b, w)

    def piece(j, q):
        _, a, n, b, w = CUTS[j]
        return pl.ds(a, n), pl.ds(pl.multiple_of(b + q * (w // SIDE), 128), w // SIDE)

    def part(j):
        _, a, n, b, w = CUTS[j]
        return pl.ds(a, n), pl.ds(b // SIDE, w // SIDE)

    for j in range(CHUNKS):
        R, C = cut(j)
        for o in range(2):
            send(
                kd.at[1 - c, o, :, :, R, C], r0.at[o, :, :, R, C],
                send_sem.at[0], sem0.at[j, o], sibling,
            )
    loads[1].wait()
    send(gd_v, g_core, gsend_sem.at[0], gc_sem, sibling)
    for cp in loads[3:]:
        cp.start()

    @pl.when(c == 0)
    def _():
        pl.semaphore_wait(barrier, CORES * 2 * (SIDE - 1) + lower)
        greet(pair_sem, sibling)

    @pl.when(c == 1)
    def _():
        pl.semaphore_wait(pair_sem, 1)

    first = (x, y)
    second = (y, x)
    far = (ypeer, xpeer)

    def on_axis(o, q):
        return at(q, y, c) if o == 0 else at(x, q, c)

    def pairing(o, u):
        i = first[o]
        swap, mirror = i + 1 - 2 * (i % 2), 3 - i
        loc = (i + 1) % SIDE if u == 0 else i
        near, last = (swap, mirror) if u == 0 else (mirror, swap)
        base = 2 * (loc // 2)
        return dict(
            near=on_axis(o, near), last=on_axis(o, last), loc=loc,
            group=base, sent=2 - base, mate=2 * base + 1 - loc,
        )

    both = [(o, u) for o in range(2) for u in range(2)]
    pair = {ou: pairing(*ou) for ou in both}
    axis = (xpeer, ypeer)
    paired = [j for j in range(CHUNKS) if CUTS[j][0]]

    def place(j, o, u):
        return pair[o, u]["loc"] if CUTS[j][0] else first[o]

    loads[0].wait()
    for j in range(CHUNKS):
        R, C = cut(j)
        for o in range(2):
            wait(sem0.at[j, o], r0.at[o, :, :, R, C])
            acc[o, :, :, R, C] = acc[o, :, :, R, C] + r0[o, :, :, R, C]
            if CUTS[j][0]:
                for u in range(2):
                    p = pair[o, u]
                    send(
                        acc.at[o, u, pl.ds(p["sent"], 2), R, C], r1a.at[o, u, :, R, C],
                        send_sem.at[1], sem1a.at[j, o, u], p["near"],
                    )
            else:
                for p in (1, 0, 2):
                    send(
                        acc.at[o, :, (first[o] + p + 1) % SIDE, R, C], r1.at[o, p, :, R, C],
                        send_sem.at[6], sem1.at[j, o], axis[o][p],
                    )
        if j == 0:
            wait(gc_sem, g_core)
            g_x[x] = gd_v[...] + g_core[...]
            for device in xpeer:
                send(g_x.at[x], g_x.at[x], gsend_sem.at[1], gx_sem, device)
    wait(gx_sem, g_x.at[0:3])
    g_y[y] = (g_x[0] + g_x[1]) + (g_x[2] + g_x[3])
    for device in ypeer:
        send(g_y.at[y], g_y.at[y], gsend_sem.at[2], gy_sem, device)

    for j in paired:
        R, C = cut(j)
        for o, u in both:
            p = pair[o, u]
            group = pl.ds(p["group"], 2)
            wait(sem1a.at[j, o, u], r1a.at[o, u, :, R, C])
            acc[o, u, group, R, C] = acc[o, u, group, R, C] + r1a[o, u, :, R, C]
            send(
                acc.at[o, u, p["mate"], R, C], r1b.at[o, u, R, C],
                send_sem.at[2], sem1b.at[j, o, u], p["last"],
            )
    for j in range(CHUNKS):
        R, C = cut(j)
        for o in range(2):
            if CUTS[j][0]:
                for u in range(2):
                    wait(sem1b.at[j, o, u], r1b.at[o, u, R, C])
                    c2[o, u, R, C] = acc[o, u, pair[o, u]["loc"], R, C] + r1b[o, u, R, C]
            else:
                wait(sem1.at[j, o], r1.at[o, :, :, R, C])
                c2[o, :, R, C] = (acc[o, :, first[o], R, C] + r1[o, 0, :, R, C]) + (r1[o, 1, :, R, C] + r1[o, 2, :, R, C])
            for p in (1, 0, 2):
                Rq, Cq = piece(j, (second[o] + p + 1) % SIDE)
                Rp, Cp = part(j)
                send(
                    c2.at[o, :, Rq, Cq], r2.at[o, p, :, Rp, Cp],
                    send_sem.at[3], sem2.at[j, o], far[o][p],
                )

    wait(gy_sem, g_y.at[0:3])
    for cp in loads[2:]:
        cp.wait()
    g_avg = ((g_y[0] + g_y[1]) + (g_y[2] + g_y[3])) * (1.0 / NREP)
    g_mom = 0.9 * gm_v[...] + g_avg
    g_step = g_avg + 0.9 * g_mom
    gmn_out[...] = g_mom
    gstep_out[...] = g_step
    g_sq = g_step * g_step
    g_part = (g_sq[:, 0:128] + g_sq[:, 128:256]) + (g_sq[:, 256:384] + g_sq[:, 384:512])

    k_part = jnp.zeros((8, 128), jnp.float32)
    for j in range(CHUNKS):
        Rp, Cp = part(j)
        for o in range(2):
            wait(sem2.at[j, o], r2.at[o, :, :, Rp, Cp])
            Rq, Cq = piece(j, second[o])
            mean = (c2[o, :, Rq, Cq] + r2[o, 0, :, Rp, Cp]) + (r2[o, 1, :, Rp, Cp] + r2[o, 2, :, Rp, Cp])
            mean = mean * (1.0 / NREP)
            c3[o, :, Rq, Cq] = mean
            for p in (1, 0, 2):
                send(
                    c3.at[o, :, Rq, Cq], c3.at[o, :, Rq, Cq],
                    send_sem.at[4], sem3.at[j, o], far[o][p],
                )
            for u in range(2):
                step = mean[u] + 0.9 * (0.9 * km[c, o, u, place(j, o, u), Rq, Cq] + mean[u])
                square = step * step
                for a in range(0, step.shape[0], 8):
                    for b in range(0, step.shape[1], 128):
                        k_part = k_part + square[a:a + 8, b:b + 128]

    @pl.when(early)
    def _():
        pl.semaphore_wait(ready_sem, CORES * (ZS - 1 - z))

    @pl.when(z == 0)
    def _():
        for k in range(1, ZS):
            greet(go_sem, (r, k))

    @pl.when(z > 0)
    def _():
        pl.semaphore_wait(go_sem, 1)

    own_z = z * CORES + c
    own_p = x * SIDE + y
    own_d = own_z * SIDE * SIDE + own_p
    k_line = jnp.sum(k_part, axis=0, keepdims=True)
    s_z[own_z, :, 0:128] = k_line
    s_z[own_z, :, 128:256] = g_part
    at_zero = [jnp.logical_and(z == 0, r == d) for d in DIRECT]
    direct = at_zero[0]
    for here in at_zero[1:]:
        direct = jnp.logical_or(direct, here)
    for d, here in zip(DIRECT, at_zero):
        @pl.when(jnp.logical_not(here))
        def _():
            send(s_z.at[own_z, :, pl.ds(0, 128)], s_d.at[own_d], ssend_sem.at[2], sd_sem, (d, 0))

    @pl.when(direct)
    def _():
        s_d[own_d] = k_line

    for device in column:
        send(s_z.at[own_z], s_z.at[own_z], ssend_sem.at[0], sz_sem, device)

    for j in range(CHUNKS):
        R, C = cut(j)
        for o in range(2):
            wait(sem3.at[j, o], r2.at[o, :, :, part(j)[0], part(j)[1]])
            for u in range(2):
                avg[c, o, u, place(j, o, u), R, C] = c3[o, u, R, C]
            for p in (1, 0, 2):
                for u in range(2):
                    send(
                        c3.at[o, u, R, C], avg.at[c, o, u, place(j, o, u), R, C],
                        send_sem.at[5], sem4.at[j, o], axis[o][p],
                    )

    def plane_round():
        wait(sz_sem, s_z.at[0:15])
        s_all = s_z[0]
        for k in range(1, ZS * CORES):
            s_all = s_all + s_z[k]
        s_p[own_p] = s_all[:, 0:128]
        total[:, 128:256] = s_all[:, 128:256]
        for device in plane:
            skip = device[0] == DIRECT[0]
            for d in DIRECT[1:]:
                skip = jnp.logical_or(skip, device[0] == d)

            @pl.when(jnp.logical_not(jnp.logical_and(z == 0, skip)))
            def _():
                send(s_p.at[own_p], s_p.at[own_p], ssend_sem.at[1], sp_sem, device)

    def finish(side, o, j):
        R, C = cut(j)

        def block(i, carry):
            at_block = (side, o, i // SIDE, i % SIDE, R, C)
            a = avg[at_block]
            m = 0.9 * km[at_block] + a
            mom[at_block] = m
            stp[at_block] = a + 0.9 * m
            return carry
        lax.fori_loop(0, 2 * SIDE, block, 0, unroll=2)

    pl.when(z >= SLACK)(plane_round)
    for j in range(CHUNKS):
        R, C = cut(j)
        for o in range(2):
            wait(sem4.at[j, o], r1.at[o, :, :, R, C])
            blocks = avg.at[c, o, :, :, R, C]
            send(blocks, blocks, send_sem.at[7], sem5.at[j, o], sibling)
    pl.when(z < SLACK)(plane_round)
    for j in range(CHUNKS):
        for o in range(2):
            finish(c, o, j)
    for j in range(CHUNKS):
        R, C = cut(j)
        for o in range(2):
            wait(sem5.at[j, o], r0.at[o, :, :, R, C])
            finish(1 - c, o, j)

    def sent(sem, refs):
        for ref in refs:
            wait(sem, ref)

    straight = [j for j in range(CHUNKS) if not CUTS[j][0]]
    sent(send_sem.at[1], [r1a.at[:, :, :, cut(j)[0], cut(j)[1]] for j in paired])
    sent(send_sem.at[2], [r1b.at[:, :, cut(j)[0], cut(j)[1]] for j in paired])
    sent(send_sem.at[6], [r1.at[:, :, :, cut(j)[0], cut(j)[1]] for j in straight])
    wait(send_sem.at[5], r1)
    wait(send_sem.at[0], r0)
    wait(send_sem.at[3], r2)
    wait(send_sem.at[4], r2)
    wait(send_sem.at[7], r0)
    wait(gsend_sem.at[0], g_core)
    wait(gsend_sem.at[1], g_x.at[0:3])
    wait(gsend_sem.at[2], g_y.at[0:3])
    wait(ssend_sem.at[0], s_z.at[0:15])
    wait(ssend_sem.at[1], s_p.at[0:15 - len(DIRECT)])
    for d, here in zip(DIRECT, at_zero):
        skipped = jnp.logical_and(z == 0, jnp.logical_and(c == d % CORES, jnp.logical_not(here)))

        @pl.when(jnp.logical_not(skipped))
        def _():
            wait(ssend_sem.at[1], s_p.at[0])

        @pl.when(jnp.logical_not(here))
        def _():
            wait(ssend_sem.at[2], s_d.at[0])

    @pl.when(jnp.logical_not(direct))
    def _():
        wait(sp_sem, s_p.at[0:15])
        s_all = s_p[0]
        for k in range(1, SIDE * SIDE):
            s_all = s_all + s_p[k]
        total[:, 0:128] = s_all

    @pl.when(direct)
    def _():
        wait(sd_sem, s_d.at[0:255])
        column_sums = s_d[0:16]
        for k in range(1, ZS * CORES):
            column_sums = column_sums + s_d[16 * k:16 * k + 16]
        s_all = column_sums[0]
        for k in range(1, SIDE * SIDE):
            s_all = s_all + column_sums[k]
        total[:, 0:128] = s_all


def tail_kernel(
    mom, stp, kp, total, gmn, g_step, gp_hbm, kn_out, kmn_out, gn_out, gmn_out, kn, gn, gp, sem
):
    load = pltpu.make_async_copy(gp_hbm, gp, sem.at[0])
    load.start()
    copies = [
        pltpu.make_async_copy(mom, kmn_out, sem.at[1]),
        pltpu.make_async_copy(gmn, gmn_out, sem.at[2]),
    ]
    for cp in copies:
        cp.start()
    k_sum = jnp.full((8, 128), jnp.sum(total[:, 0:128]), jnp.float32)
    k_scale = 0.7 / jnp.sqrt(k_sum / (D * KV) + 1e-06)
    k_scale = jnp.concatenate([k_scale] * (KV // 128), axis=1)
    k_scale = jnp.concatenate([k_scale] * (BR // 8), axis=0)
    for t in range(CORES * 2 * 2):
        blocks = (t // 4, t // 2 % 2, t % 2)

        def block(i, carry):
            kn[blocks + (i,)] = kp[blocks + (i,)] - stp[blocks + (i,)] * k_scale
            return carry
        lax.fori_loop(0, SIDE, block, 0)
        cp = pltpu.make_async_copy(kn.at[blocks], kn_out.at[blocks], sem.at[4 + t])
        cp.start()
        copies.append(cp)
    load.wait()
    g_sum = jnp.full((1, ROWS), jnp.sum(total[:, 128:256]) * (1.0 / CORES), jnp.float32)
    gn[...] = gp[...] - g_step[...] * (0.7 / jnp.sqrt(g_sum / D + 1e-06))
    cp = pltpu.make_async_copy(gn, gn_out, sem.at[3])
    cp.start()
    copies.append(cp)
    for cp in copies:
        cp.wait()


def on_device(key_delta, gain_delta, key_params, key_moment, gain_params, gain_moment):
    f32 = jnp.float32
    dma = pltpu.SemaphoreType.DMA
    signal = pltpu.SemaphoreType.REGULAR
    vector = pltpu.VMEM
    hbm = pl.BlockSpec(memory_space=pltpu.HBM)
    vmem = pl.BlockSpec(memory_space=pltpu.VMEM)
    whole = jax.ShapeDtypeStruct(SHAPE, f32)
    line = jax.ShapeDtypeStruct((1, ROWS), f32)
    hold = lambda a: pltpu.with_memory_space_constraint(a, pltpu.HBM)
    rows = lambda a: a.reshape(SHAPE)
    inputs = (rows(key_delta), gain_delta, rows(key_params), rows(key_moment), gain_moment.reshape(1, ROWS))
    parts = pl.pallas_call(
        comm_kernel,
        out_shape=(whole, whole, whole, jax.ShapeDtypeStruct((1, 256), f32), line, line),
        in_specs=[hbm] * 5,
        out_specs=[vmem] * 6,
        scratch_shapes=[
            vector(OWN, f32),
            vector(OWN, f32),
            vector((2, 2, 2, BR, KV), f32),
            vector((2, 2, BR, KV), f32),
            vector((2, 3, 2, BR, KV), f32),
            vector((2, 2, BR, KV), f32),
            vector((2, 3, 2, BR, KV // SIDE), f32),
            vector((2, 2, BR, KV), f32),
            vector(SHAPE, f32),
            vector(SHAPE, f32),
            vector((1, ROWS), f32),
            vector((1, ROWS), f32),
            vector((1, ROWS), f32),
            vector((4, 1, ROWS), f32),
            vector((4, 1, ROWS), f32),
            vector((16, 1, 256), f32),
            vector((16, 1, 128), f32),
            vector((256, 1, 128), f32),
            dma((5,)),
            dma((8,)),
            dma((CHUNKS, 2)),
            dma((CHUNKS, 2, 2)),
            dma((CHUNKS, 2, 2)),
            dma((CHUNKS, 2)),
            dma((CHUNKS, 2)),
            dma((CHUNKS, 2)),
            dma((CHUNKS, 2)),
            dma((CHUNKS, 2)),
            dma((3,)),
            dma,
            dma,
            dma,
            dma((3,)),
            dma,
            dma,
            dma,
            signal,
            signal,
            signal,
        ],
        compiler_params=pltpu.CompilerParams(
            collective_id=0, has_side_effects=True, vmem_limit_bytes=32 << 20
        ),
        name="worker_mean",
    )(*map(hold, inputs))
    kn, kmn, gn, gmn = pl.pallas_call(
        tail_kernel,
        out_shape=(whole, whole, line, line),
        in_specs=[vmem] * 6 + [hbm],
        out_specs=[hbm] * 4,
        scratch_shapes=[
            vector(SHAPE, f32),
            vector((1, ROWS), f32),
            vector((1, ROWS), f32),
            dma((4 + CORES * 2 * 2,)),
        ],
        compiler_params=pltpu.CompilerParams(vmem_limit_bytes=32 << 20),
        name="apply_step",
    )(*parts, hold(gain_params.reshape(1, ROWS)))
    return kn.reshape(ROWS, KV), kmn.reshape(ROWS, KV), gn.reshape(ROWS), gmn.reshape(ROWS)


def solution(mesh):
    return jax.shard_map(
        on_device,
        mesh=mesh,
        in_specs=(
            P("replica", "fsdp", None),
            P("replica", "fsdp"),
            P("fsdp", None),
            P("fsdp", None),
            P("fsdp"),
            P("fsdp"),
        ),
        out_specs=(P("fsdp", None), P("fsdp", None), P("fsdp"), P("fsdp")),
        check_vma=False,
    )
```

```python
import jax
import jax.numpy as jnp
from jax import lax
from jax.experimental import pallas as pl
from jax.experimental.pallas import tpu as pltpu
from jax.sharding import PartitionSpec as P

D = 4096
KV = 1024
NREP = 32
SIDE, CORES, ZS = 4, 2, 8
ROWS = D // ZS
BR = ROWS // (CORES * 2 * 2 * SIDE)
SHAPE = (CORES, 2, 2, SIDE, BR, KV)
OWN = SHAPE[1:]
CUTS = [(True, 0, 8, 0, 512), (True, 0, 8, 512, 512), (True, 8, 8, 0, 512), (False, 8, 8, 512, 512)]
CHUNKS = len(CUTS)
EARLY = 1
SLACK = 1
DIRECT = (1, 2, 8)
MESH = pl.DeviceIdType.MESH


def comm_kernel(
    kd, gd, kp_hbm, km_hbm, gm_hbm,
    mom, stp, kp, total, gmn_out, gstep_out,
    acc, r0, r1a, r1b, r1, c2, r2, c3, avg, km,
    gd_v, gm_v, g_core, g_x, g_y, s_z, s_p, s_d,
    load_sem, send_sem, sem0, sem1a, sem1b, sem1, sem2, sem3, sem4, sem5,
    gsend_sem, gc_sem, gx_sem, gy_sem, ssend_sem, sz_sem, sp_sem, sd_sem, ready_sem, go_sem,
):
    r = lax.axis_index("replica")
    z = lax.axis_index("fsdp")
    x = r // (SIDE * CORES)
    y = (r // CORES) % SIDE
    c = r % CORES

    def at(px, py, pc):
        return ((px * SIDE + py) * CORES + pc, z)

    sibling = at(x, y, 1 - c)
    xpeer = [at((x + p) % SIDE, y, c) for p in (1, 2, 3)]
    ypeer = [at(x, (y + p) % SIDE, c) for p in (1, 2, 3)]
    away = (2, 1, 3, 0)
    plane = [at((x + p) % SIDE, (y + q) % SIDE, c) for p in away for q in away if p or q]
    column = [
        (at(x, y, (c + q) % 2)[0], (z + p) % ZS)
        for p in (4, 3, 5, 2, 6, 1, 7, 0) for q in (1, 0) if p or q
    ]
    barrier = pltpu.get_barrier_semaphore()

    def greet(sem, device):
        pl.semaphore_signal(sem, inc=1, device_id=device, device_id_type=MESH)

    def greet_column(sem, k):
        for q in range(CORES):
            greet(sem, (at(x, y, q)[0], k))

    early = z < EARLY
    for device in [sibling] + xpeer + ypeer:
        greet(barrier, device)
    for k in range(1, ZS):
        pl.when(jnp.logical_and(k > z, early))(lambda: greet_column(barrier, k))

    loads = [
        pltpu.make_async_copy(kd.at[c], acc, load_sem.at[0]),
        pltpu.make_async_copy(gd, gd_v, load_sem.at[1]),
        pltpu.make_async_copy(gm_hbm, gm_v, load_sem.at[2]),
        pltpu.make_async_copy(km_hbm, km, load_sem.at[3]),
        pltpu.make_async_copy(kp_hbm, kp, load_sem.at[4]),
    ]
    for cp in loads[:3]:
        cp.start()

    def send(src, dst, ssem, rsem, device):
        pltpu.make_async_remote_copy(
            src_ref=src, dst_ref=dst, send_sem=ssem, recv_sem=rsem,
            device_id=device, device_id_type=MESH,
        ).start()

    def wait(sem, like):
        pltpu.make_async_copy(like, like, sem).wait()

    pl.semaphore_wait(barrier, 1 + 2 * (SIDE - 1) + CORES * jnp.minimum(z, EARLY))

    def cut(j):
        _, a, n, b, w = CUTS[j]
        return pl.ds(a, n), pl.ds(b, w)

    def piece(j, q):
        _, a, n, b, w = CUTS[j]
        return pl.ds(a, n), pl.ds(pl.multiple_of(b + q * (w // SIDE), 128), w // SIDE)

    def part(j):
        _, a, n, b, w = CUTS[j]
        return pl.ds(a, n), pl.ds(b // SIDE, w // SIDE)

    for j in range(CHUNKS):
        R, C = cut(j)
        for o in range(2):
            send(
                kd.at[1 - c, o, :, :, R, C], r0.at[o, :, :, R, C],
                send_sem.at[0], sem0.at[j, o], sibling,
            )
    loads[1].wait()
    send(gd_v, g_core, gsend_sem.at[0], gc_sem, sibling)
    for cp in loads[3:]:
        cp.start()
    for k in range(EARLY):
        pl.when(k < z)(lambda: greet_column(ready_sem, k))

    first = (x, y)
    second = (y, x)
    far = (ypeer, xpeer)

    def on_axis(o, q):
        return at(q, y, c) if o == 0 else at(x, q, c)

    def pairing(o, u):
        i = first[o]
        swap, mirror = i + 1 - 2 * (i % 2), 3 - i
        loc = (i + 1) % SIDE if u == 0 else i
        near, last = (swap, mirror) if u == 0 else (mirror, swap)
        base = 2 * (loc // 2)
        return dict(
            near=on_axis(o, near), last=on_axis(o, last), loc=loc,
            group=base, sent=2 - base, mate=2 * base + 1 - loc,
        )

    both = [(o, u) for o in range(2) for u in range(2)]
    pair = {ou: pairing(*ou) for ou in both}
    axis = (xpeer, ypeer)
    paired = [j for j in range(CHUNKS) if CUTS[j][0]]

    def place(j, o, u):
        return pair[o, u]["loc"] if CUTS[j][0] else first[o]

    loads[0].wait()
    for j in range(CHUNKS):
        R, C = cut(j)
        for o in range(2):
            wait(sem0.at[j, o], r0.at[o, :, :, R, C])
            acc[o, :, :, R, C] = acc[o, :, :, R, C] + r0[o, :, :, R, C]
            if CUTS[j][0]:
                for u in range(2):
                    p = pair[o, u]
                    send(
                        acc.at[o, u, pl.ds(p["sent"], 2), R, C], r1a.at[o, u, :, R, C],
                        send_sem.at[1], sem1a.at[j, o, u], p["near"],
                    )
            else:
                for p in (1, 0, 2):
                    send(
                        acc.at[o, :, (first[o] + p + 1) % SIDE, R, C], r1.at[o, p, :, R, C],
                        send_sem.at[6], sem1.at[j, o], axis[o][p],
                    )
        if j == 0:
            wait(gc_sem, g_core)
            g_x[x] = gd_v[...] + g_core[...]
            for device in xpeer:
                send(g_x.at[x], g_x.at[x], gsend_sem.at[1], gx_sem, device)
    wait(gx_sem, g_x.at[0:3])
    g_y[y] = (g_x[0] + g_x[1]) + (g_x[2] + g_x[3])
    for device in ypeer:
        send(g_y.at[y], g_y.at[y], gsend_sem.at[2], gy_sem, device)

    for j in paired:
        R, C = cut(j)
        for o, u in both:
            p = pair[o, u]
            group = pl.ds(p["group"], 2)
            wait(sem1a.at[j, o, u], r1a.at[o, u, :, R, C])
            acc[o, u, group, R, C] = acc[o, u, group, R, C] + r1a[o, u, :, R, C]
            send(
                acc.at[o, u, p["mate"], R, C], r1b.at[o, u, R, C],
                send_sem.at[2], sem1b.at[j, o, u], p["last"],
            )
    for j in range(CHUNKS):
        R, C = cut(j)
        for o in range(2):
            if CUTS[j][0]:
                for u in range(2):
                    wait(sem1b.at[j, o, u], r1b.at[o, u, R, C])
                    c2[o, u, R, C] = acc[o, u, pair[o, u]["loc"], R, C] + r1b[o, u, R, C]
            else:
                wait(sem1.at[j, o], r1.at[o, :, :, R, C])
                c2[o, :, R, C] = (acc[o, :, first[o], R, C] + r1[o, 0, :, R, C]) + (r1[o, 1, :, R, C] + r1[o, 2, :, R, C])
            for p in (1, 0, 2):
                Rq, Cq = piece(j, (second[o] + p + 1) % SIDE)
                Rp, Cp = part(j)
                send(
                    c2.at[o, :, Rq, Cq], r2.at[o, p, :, Rp, Cp],
                    send_sem.at[3], sem2.at[j, o], far[o][p],
                )

    wait(gy_sem, g_y.at[0:3])
    for cp in loads[2:]:
        cp.wait()
    g_avg = ((g_y[0] + g_y[1]) + (g_y[2] + g_y[3])) * (1.0 / NREP)
    g_mom = 0.9 * gm_v[...] + g_avg
    g_step = g_avg + 0.9 * g_mom
    gmn_out[...] = g_mom
    gstep_out[...] = g_step
    g_sq = g_step * g_step
    g_part = (g_sq[:, 0:128] + g_sq[:, 128:256]) + (g_sq[:, 256:384] + g_sq[:, 384:512])

    @pl.when(early)
    def _():
        pl.semaphore_wait(ready_sem, CORES * (ZS - 1 - z))

    k_part = jnp.zeros((8, 128), jnp.float32)
    for j in range(CHUNKS):
        Rp, Cp = part(j)
        for o in range(2):
            wait(sem2.at[j, o], r2.at[o, :, :, Rp, Cp])
            Rq, Cq = piece(j, second[o])
            mean = (c2[o, :, Rq, Cq] + r2[o, 0, :, Rp, Cp]) + (r2[o, 1, :, Rp, Cp] + r2[o, 2, :, Rp, Cp])
            mean = mean * (1.0 / NREP)
            c3[o, :, Rq, Cq] = mean
            for p in (1, 0, 2):
                send(
                    c3.at[o, :, Rq, Cq], c3.at[o, :, Rq, Cq],
                    send_sem.at[4], sem3.at[j, o], far[o][p],
                )
            for u in range(2):
                step = mean[u] + 0.9 * (0.9 * km[c, o, u, place(j, o, u), Rq, Cq] + mean[u])
                square = step * step
                for a in range(0, step.shape[0], 8):
                    for b in range(0, step.shape[1], 128):
                        k_part = k_part + square[a:a + 8, b:b + 128]
        if j == 0:
            @pl.when(z == 0)
            def _():
                for k in range(1, ZS):
                    greet(go_sem, (r, k))

    @pl.when(z > 0)
    def _():
        pl.semaphore_wait(go_sem, 1)

    own_z = z * CORES + c
    own_p = x * SIDE + y
    own_d = own_z * SIDE * SIDE + own_p
    k_line = jnp.sum(k_part, axis=0, keepdims=True)
    s_z[own_z, :, 0:128] = k_line
    s_z[own_z, :, 128:256] = g_part
    at_zero = [jnp.logical_and(z == 0, r == d) for d in DIRECT]
    direct = at_zero[0]
    for here in at_zero[1:]:
        direct = jnp.logical_or(direct, here)
    for d, here in zip(DIRECT, at_zero):
        @pl.when(jnp.logical_not(here))
        def _():
            send(s_z.at[own_z, :, pl.ds(0, 128)], s_d.at[own_d], ssend_sem.at[2], sd_sem, (d, 0))

    @pl.when(direct)
    def _():
        s_d[own_d] = k_line

    for device in column:
        send(s_z.at[own_z], s_z.at[own_z], ssend_sem.at[0], sz_sem, device)

    for j in range(CHUNKS):
        R, C = cut(j)
        for o in range(2):
            wait(sem3.at[j, o], r2.at[o, :, :, part(j)[0], part(j)[1]])
            for u in range(2):
                avg[c, o, u, place(j, o, u), R, C] = c3[o, u, R, C]
            for p in (1, 0, 2):
                for u in range(2):
                    send(
                        c3.at[o, u, R, C], avg.at[c, o, u, place(j, o, u), R, C],
                        send_sem.at[5], sem4.at[j, o], axis[o][p],
                    )

    def plane_round():
        wait(sz_sem, s_z.at[0:15])
        s_all = s_z[0]
        for k in range(1, ZS * CORES):
            s_all = s_all + s_z[k]
        s_p[own_p] = s_all[:, 0:128]
        total[:, 128:256] = s_all[:, 128:256]
        for device in plane:
            skip = device[0] == DIRECT[0]
            for d in DIRECT[1:]:
                skip = jnp.logical_or(skip, device[0] == d)

            @pl.when(jnp.logical_not(jnp.logical_and(z == 0, skip)))
            def _():
                send(s_p.at[own_p], s_p.at[own_p], ssend_sem.at[1], sp_sem, device)

    def finish(side, o, j):
        R, C = cut(j)

        def block(i, carry):
            at_block = (side, o, i // SIDE, i % SIDE, R, C)
            a = avg[at_block]
            m = 0.9 * km[at_block] + a
            mom[at_block] = m
            stp[at_block] = a + 0.9 * m
            return carry
        lax.fori_loop(0, 2 * SIDE, block, 0, unroll=2)

    pl.when(z >= SLACK)(plane_round)
    for j in range(CHUNKS):
        R, C = cut(j)
        for o in range(2):
            wait(sem4.at[j, o], r1.at[o, :, :, R, C])
            blocks = avg.at[c, o, :, :, R, C]
            send(blocks, blocks, send_sem.at[7], sem5.at[j, o], sibling)
    pl.when(z < SLACK)(plane_round)
    for j in range(CHUNKS):
        for o in range(2):
            finish(c, o, j)
    for j in range(CHUNKS):
        R, C = cut(j)
        for o in range(2):
            wait(sem5.at[j, o], r0.at[o, :, :, R, C])
            finish(1 - c, o, j)

    def sent(sem, refs):
        for ref in refs:
            wait(sem, ref)

    straight = [j for j in range(CHUNKS) if not CUTS[j][0]]
    sent(send_sem.at[1], [r1a.at[:, :, :, cut(j)[0], cut(j)[1]] for j in paired])
    sent(send_sem.at[2], [r1b.at[:, :, cut(j)[0], cut(j)[1]] for j in paired])
    sent(send_sem.at[6], [r1.at[:, :, :, cut(j)[0], cut(j)[1]] for j in straight])
    wait(send_sem.at[5], r1)
    wait(send_sem.at[0], r0)
    wait(send_sem.at[3], r2)
    wait(send_sem.at[4], r2)
    wait(send_sem.at[7], r0)
    wait(gsend_sem.at[0], g_core)
    wait(gsend_sem.at[1], g_x.at[0:3])
    wait(gsend_sem.at[2], g_y.at[0:3])
    wait(ssend_sem.at[0], s_z.at[0:15])
    wait(ssend_sem.at[1], s_p.at[0:15 - len(DIRECT)])
    for d, here in zip(DIRECT, at_zero):
        skipped = jnp.logical_and(z == 0, jnp.logical_and(c == d % CORES, jnp.logical_not(here)))

        @pl.when(jnp.logical_not(skipped))
        def _():
            wait(ssend_sem.at[1], s_p.at[0])

        @pl.when(jnp.logical_not(here))
        def _():
            wait(ssend_sem.at[2], s_d.at[0])

    @pl.when(jnp.logical_not(direct))
    def _():
        wait(sp_sem, s_p.at[0:15])
        s_all = s_p[0]
        for k in range(1, SIDE * SIDE):
            s_all = s_all + s_p[k]
        total[:, 0:128] = s_all

    @pl.when(direct)
    def _():
        wait(sd_sem, s_d.at[0:255])
        column_sums = s_d[0:16]
        for k in range(1, ZS * CORES):
            column_sums = column_sums + s_d[16 * k:16 * k + 16]
        s_all = column_sums[0]
        for k in range(1, SIDE * SIDE):
            s_all = s_all + column_sums[k]
        total[:, 0:128] = s_all


def tail_kernel(
    mom, stp, kp, total, gmn, g_step, gp_hbm, kn_out, kmn_out, gn_out, gmn_out, kn, gn, gp, sem
):
    load = pltpu.make_async_copy(gp_hbm, gp, sem.at[0])
    load.start()
    copies = [
        pltpu.make_async_copy(mom, kmn_out, sem.at[1]),
        pltpu.make_async_copy(gmn, gmn_out, sem.at[2]),
    ]
    for cp in copies:
        cp.start()
    k_sum = jnp.full((8, 128), jnp.sum(total[:, 0:128]), jnp.float32)
    k_scale = 0.7 / jnp.sqrt(k_sum / (D * KV) + 1e-06)
    k_scale = jnp.concatenate([k_scale] * (KV // 128), axis=1)
    k_scale = jnp.concatenate([k_scale] * (BR // 8), axis=0)
    for t in range(CORES * 2 * 2):
        blocks = (t // 4, t // 2 % 2, t % 2)

        def block(i, carry):
            kn[blocks + (i,)] = kp[blocks + (i,)] - stp[blocks + (i,)] * k_scale
            return carry
        lax.fori_loop(0, SIDE, block, 0)
        cp = pltpu.make_async_copy(kn.at[blocks], kn_out.at[blocks], sem.at[4 + t])
        cp.start()
        copies.append(cp)
    load.wait()
    g_sum = jnp.full((1, ROWS), jnp.sum(total[:, 128:256]) * (1.0 / CORES), jnp.float32)
    gn[...] = gp[...] - g_step[...] * (0.7 / jnp.sqrt(g_sum / D + 1e-06))
    cp = pltpu.make_async_copy(gn, gn_out, sem.at[3])
    cp.start()
    copies.append(cp)
    for cp in copies:
        cp.wait()


def on_device(key_delta, gain_delta, key_params, key_moment, gain_params, gain_moment):
    f32 = jnp.float32
    dma = pltpu.SemaphoreType.DMA
    signal = pltpu.SemaphoreType.REGULAR
    vector = pltpu.VMEM
    hbm = pl.BlockSpec(memory_space=pltpu.HBM)
    vmem = pl.BlockSpec(memory_space=pltpu.VMEM)
    whole = jax.ShapeDtypeStruct(SHAPE, f32)
    line = jax.ShapeDtypeStruct((1, ROWS), f32)
    hold = lambda a: pltpu.with_memory_space_constraint(a, pltpu.HBM)
    rows = lambda a: a.reshape(SHAPE)
    inputs = (rows(key_delta), gain_delta, rows(key_params), rows(key_moment), gain_moment.reshape(1, ROWS))
    parts = pl.pallas_call(
        comm_kernel,
        out_shape=(whole, whole, whole, jax.ShapeDtypeStruct((1, 256), f32), line, line),
        in_specs=[hbm] * 5,
        out_specs=[vmem] * 6,
        scratch_shapes=[
            vector(OWN, f32),
            vector(OWN, f32),
            vector((2, 2, 2, BR, KV), f32),
            vector((2, 2, BR, KV), f32),
            vector((2, 3, 2, BR, KV), f32),
            vector((2, 2, BR, KV), f32),
            vector((2, 3, 2, BR, KV // SIDE), f32),
            vector((2, 2, BR, KV), f32),
            vector(SHAPE, f32),
            vector(SHAPE, f32),
            vector((1, ROWS), f32),
            vector((1, ROWS), f32),
            vector((1, ROWS), f32),
            vector((4, 1, ROWS), f32),
            vector((4, 1, ROWS), f32),
            vector((16, 1, 256), f32),
            vector((16, 1, 128), f32),
            vector((256, 1, 128), f32),
            dma((5,)),
            dma((8,)),
            dma((CHUNKS, 2)),
            dma((CHUNKS, 2, 2)),
            dma((CHUNKS, 2, 2)),
            dma((CHUNKS, 2)),
            dma((CHUNKS, 2)),
            dma((CHUNKS, 2)),
            dma((CHUNKS, 2)),
            dma((CHUNKS, 2)),
            dma((3,)),
            dma,
            dma,
            dma,
            dma((3,)),
            dma,
            dma,
            dma,
            signal,
            signal,
        ],
        compiler_params=pltpu.CompilerParams(
            collective_id=0, has_side_effects=True, vmem_limit_bytes=32 << 20
        ),
        name="worker_mean",
    )(*map(hold, inputs))
    kn, kmn, gn, gmn = pl.pallas_call(
        tail_kernel,
        out_shape=(whole, whole, line, line),
        in_specs=[vmem] * 6 + [hbm],
        out_specs=[hbm] * 4,
        scratch_shapes=[
            vector(SHAPE, f32),
            vector((1, ROWS), f32),
            vector((1, ROWS), f32),
            dma((4 + CORES * 2 * 2,)),
        ],
        compiler_params=pltpu.CompilerParams(vmem_limit_bytes=32 << 20),
        name="apply_step",
    )(*parts, hold(gain_params.reshape(1, ROWS)))
    return kn.reshape(ROWS, KV), kmn.reshape(ROWS, KV), gn.reshape(ROWS), gmn.reshape(ROWS)


def solution(mesh):
    return jax.shard_map(
        on_device,
        mesh=mesh,
        in_specs=(
            P("replica", "fsdp", None),
            P("replica", "fsdp"),
            P("fsdp", None),
            P("fsdp", None),
            P("fsdp"),
            P("fsdp"),
        ),
        out_specs=(P("fsdp", None), P("fsdp", None), P("fsdp"), P("fsdp")),
        check_vma=False,
    )
```
